512 devices in a mesh: ctx: 32 (over z, x), head: 16 (over y, core).
Axes of the slice: x: 4, y: 8, z: 8, core: 2. Of those that a mesh axis runs over, the one named last changes fastest.
Arguments:
- queries: bfloat16 [8192, 4096], P('ctx', 'head'), may hold values from -5 to 5
- keys: bfloat16 [8192, 4096], P('ctx', 'head'), may hold values from -5 to 5
- values: bfloat16 [8192, 4096], P('ctx', 'head'), may hold values from -6 to 6
- grad_out: bfloat16 [8192, 4096], P('ctx', 'head'), may hold values from -6 to 6
- out_weight: bfloat16 [4096, 4096], P(None, 'head'), may hold values from -0.09375 to 0.09375
- doc_lengths: int32 [16], replicated, may hold values from 1 to 513, 8192 in all
- strata: int32 [16], replicated, may hold values from 0 to 7
- mask_level: int32 [8192], P('ctx'), may hold values from 0 to 7
Outputs:
- query_grad: bfloat16 [8192, 4096], P('ctx', 'head')
- key_grad: bfloat16 [8192, 4096], P('ctx', 'head')
- value_grad: bfloat16 [8192, 4096], P('ctx', 'head')
- out_weight_grad: float32 [4096, 4096], P('ctx', 'head')
The draws below stay inside these ranges and needn't reach their ends.
Inputs may be any that keep to these rules, and one draw needn't show every extreme that they name: `doc_lengths`: the lengths sum to 8192; the longest document has exactly 513 tokens.
All inputs are finite; a program needn't handle non-finite values.
Results may differ from the reference program's by a relative error of at most 0.011.
Values may be sent and summed in bfloat16 or wider, within the bound.
A program may use at most 64 MiB of HBM per device.

```python
import math
import jax
import jax.numpy as jnp
import numpy as np
from jax import lax

D = 4096
HD = 128
HEADS = 32
TOK_DEV = 256
SEQ = 8192
DOC_MAX = 513
NDOCS = 16
STRATA = 8


def draw_queries(key, part):
    key = jax.random.fold_in(key, 1)
    shape = (SEQ, HEADS * HD)
    base = jnp.clip(jax.random.normal(key, shape, jnp.float32), -4.0, 4.0)
    return base.astype(jnp.bfloat16)


def draw_keys(key, part):
    key = jax.random.fold_in(key, 2)
    shape = (SEQ, HEADS * HD)
    base = jnp.clip(jax.random.normal(key, shape, jnp.float32), -4.0, 4.0)
    return base.astype(jnp.bfloat16)


def plant(array, stream_key, smallest, top_value):
    place = [jax.random.randint(jax.random.fold_in(stream_key, axis), (), 0, length) for axis, length in enumerate(array.shape)]
    widest = array.shape.index(max(array.shape))
    beside = place[:widest] + [(place[widest] + 1) % array.shape[widest]] + place[widest + 1:]
    return array.at[tuple(place)].set(smallest).at[tuple(beside)].set(top_value)


def strengthened(array, stream_key, source, target, blocks, factor):
    def block_of(axis_at):
        return (jnp.arange(array.shape[axis_at]) // (array.shape[axis_at] // blocks)).reshape((-1,) + (1,) * (array.ndim - 1 - axis_at))

    one_side = jax.random.permutation(stream_key, blocks)[block_of(target)]
    other_side = (block_of(target) + blocks // 2) % blocks
    return jnp.where((block_of(source) == one_side) | (block_of(source) == other_side), factor * array, array)


def levels(stream_key, shape, cuts, least, top_value):
    factor_of = 1.0
    for position, shards_of in cuts:
        steps = jax.random.uniform(jax.random.fold_in(jax.random.fold_in(stream_key, 6), position), (shards_of,), jnp.float32, least / len(cuts), top_value / len(cuts))
        factor_of = factor_of * jnp.repeat(jnp.exp(steps), shape[position] // shards_of).reshape((-1,) + (1,) * (len(shape) - 1 - position))
    return factor_of


def length_profile(number_of, total, bound, skew):
    weights = [(1 << 20) // math.isqrt(standing ** skew) + 1 for standing in range(2, number_of + 1)]
    rest, given = total - bound - (number_of - 1), [1] * (number_of - 1)
    while rest > 0:
        movable = [i for i in range(number_of - 1) if given[i] < bound]
        mass, left = sum([weights[i] for i in movable]), rest
        for i in movable:
            more = min(bound - given[i], max(1, left * weights[i] // mass), rest)
            given[i] = given[i] + more
            rest = rest - more
    return np.array([bound] + given)


def ragged_sizes(key, count, total, bound, slope):
    if count == 2:
        one = jax.random.randint(key, (), max(1, total - bound), min(bound, total - 1) + 1)
        return jnp.stack([one, total - one])
    tallies = jnp.asarray(length_profile(count, total, bound, slope), jnp.int32)
    couples = (count - 1) // 2
    giver, receiver = tallies[1:1 + 2 * couples:2], tallies[2:2 + 2 * couples:2]
    slack = jnp.minimum(giver - 1, bound - receiver)
    moved = jax.random.randint(jax.random.fold_in(key, 1), (couples,), 0, 1 << 20) % (slack + 1)
    tallies = tallies.at[1:1 + 2 * couples:2].set(giver - moved).at[2:2 + 2 * couples:2].set(receiver + moved)
    return tallies[jax.random.permutation(jax.random.fold_in(key, 2), count)]


def centred(stream_key, dims, scale, reach, pieces=(), held_as=jnp.bfloat16):
    values = scale * jax.random.normal(stream_key, dims, jnp.float32)
    if pieces:
        values = values * levels(stream_key, dims, pieces, -0.22, 0.18)
    return jnp.clip(values, -reach, reach).astype(held_as)


def noise_with(own_key, shape, spread, reach, pieces, heavy, kind=jnp.bfloat16):
    drawn = spread * jax.random.normal(own_key, shape, jnp.float32)
    if pieces:
        drawn = drawn * levels(own_key, shape, pieces, -0.22, 0.18)
    return jnp.clip(strengthened(drawn, jax.random.fold_in(own_key, 3), *heavy), -reach, reach).astype(kind)


def setup_inputs(seed: int = 0) -> dict:
    key_of = jax.random.split(jax.random.key(seed), 9)
    return {
        "queries": draw_queries(jax.random.fold_in(key_of[8], 71), 0),
        "keys": draw_keys(jax.random.fold_in(key_of[8], 71), 0),
        "values": centred(key_of[2], (SEQ, HEADS * HD), 1.0, 6.0, ((0, 32), (1, 16))),
        "grad_out": noise_with(key_of[3], (SEQ, D), 1.0, 6.0, ((0, 32), (1, 16)), (0, 1, 32, 2.75)),
        "out_weight": centred(key_of[4], (D, HEADS * HD), D ** -0.5, 0.09375, ((1, 16),)),
        "doc_lengths": ragged_sizes(key_of[5], NDOCS, SEQ, DOC_MAX, 2).astype(jnp.int32),
        "strata": plant(jax.random.randint(key_of[6], (NDOCS,), 0, STRATA), jax.random.fold_in(key_of[6], 1), 0, STRATA - 1).astype(jnp.int32),
        "mask_level": plant(jax.random.randint(key_of[7], (SEQ,), 0, STRATA), jax.random.fold_in(key_of[7], 1), 0, STRATA - 1).astype(jnp.int32),
    }


def document_ids(doc_lengths):
    doc_ends = jnp.cumsum(doc_lengths)
    positions = jnp.arange(SEQ, dtype=jnp.int32)
    return jnp.sum((doc_ends[None, :] <= positions[:, None]).astype(jnp.int32), axis=1).astype(jnp.int32)


def reference(queries, keys, values, grad_out, out_weight, doc_lengths, strata, mask_level):
    docs = document_ids(doc_lengths)
    stratum = strata[docs]
    token_weight = (mask_level < stratum + 1).astype(jnp.float32) * (STRATA / (stratum + 1).astype(jnp.float32))
    attn_grad = (token_weight[:, None] * jnp.dot(grad_out, out_weight, preferred_element_type=jnp.float32)).astype(jnp.bfloat16)
    margin = 2 * TOK_DEV
    span = 5 * TOK_DEV
    score_scale = HD ** -0.5
    key_padded = jnp.pad(keys, ((margin, margin), (0, 0)))
    value_padded = jnp.pad(values, ((margin, margin), (0, 0)))
    docs_padded = jnp.pad(docs, (margin, margin), constant_values=-1)

    def block_step(index, state):
        query_sum, output, key_sum, value_sum = state
        start = (index * TOK_DEV).astype(jnp.int32)
        query_block = lax.dynamic_slice_in_dim(queries, start, TOK_DEV, 0).astype(jnp.float32).reshape(TOK_DEV, HEADS, HD)
        grad_block = lax.dynamic_slice_in_dim(attn_grad, start, TOK_DEV, 0).astype(jnp.float32).reshape(TOK_DEV, HEADS, HD)
        query_docs = lax.dynamic_slice_in_dim(docs, start, TOK_DEV, 0)
        key_block = lax.dynamic_slice_in_dim(key_padded, start, span, 0).astype(jnp.float32).reshape(span, HEADS, HD)
        value_block = lax.dynamic_slice_in_dim(value_padded, start, span, 0).astype(jnp.float32).reshape(span, HEADS, HD)
        key_docs = lax.dynamic_slice_in_dim(docs_padded, start, span, 0)
        same_doc = (query_docs[:, None] == key_docs[None, :])[None]
        scores = jnp.einsum("qhd,khd->hqk", query_block, key_block) * score_scale
        masked_scores = jnp.where(same_doc, scores, -1e30)
        row_max = jnp.max(masked_scores, axis=2)
        log_norm = row_max + jnp.log(jnp.sum(jnp.exp(masked_scores - row_max[:, :, None]), axis=2))
        attention = jnp.exp(masked_scores - log_norm[:, :, None])
        attention_half = attention.astype(jnp.bfloat16).astype(jnp.float32)
        block_out = jnp.einsum("hqk,khd->qhd", attention_half, value_block)
        correction = jnp.sum(grad_block * block_out, axis=2)
        dot_grad = jnp.einsum("qhd,khd->hqk", grad_block, value_block)
        score_grad = (attention * (dot_grad - correction.T[:, :, None]) * score_scale).astype(jnp.bfloat16).astype(jnp.float32)
        query_part = jnp.einsum("hqk,khd->qhd", score_grad, key_block)
        key_part = jnp.einsum("hqk,qhd->khd", score_grad, query_block).reshape(span, HEADS * HD)
        value_part = jnp.einsum("hqk,qhd->khd", attention_half, grad_block).reshape(span, HEADS * HD)
        query_sum = lax.dynamic_update_slice_in_dim(query_sum, query_part.reshape(TOK_DEV, HEADS * HD), start, 0)
        output = lax.dynamic_update_slice_in_dim(output, block_out.reshape(TOK_DEV, HEADS * HD), start, 0)
        key_sum = lax.dynamic_update_slice_in_dim(key_sum, lax.dynamic_slice_in_dim(key_sum, start, span, 0) + key_part, start, 0)
        value_sum = lax.dynamic_update_slice_in_dim(value_sum, lax.dynamic_slice_in_dim(value_sum, start, span, 0) + value_part, start, 0)
        return query_sum, output, key_sum, value_sum

    columns = HEADS * HD
    initial = (jnp.zeros((SEQ, columns), jnp.float32), jnp.zeros((SEQ, columns), jnp.float32),
               jnp.zeros((SEQ + 2 * margin, columns), jnp.float32), jnp.zeros((SEQ + 2 * margin, columns), jnp.float32))
    query_sum, output, key_sum, value_sum = lax.fori_loop(0, SEQ // TOK_DEV, block_step, initial)
    scaled_out = (token_weight[:, None] * output).astype(jnp.bfloat16)
    out_weight_grad = jnp.dot(grad_out.T, scaled_out, preferred_element_type=jnp.float32)
    return (query_sum.astype(jnp.bfloat16), key_sum[margin:margin + SEQ].astype(jnp.bfloat16),
            value_sum[margin:margin + SEQ].astype(jnp.bfloat16), out_weight_grad)
```

```python
import jax
import jax.numpy as jnp
from jax import lax
from jax.experimental import pallas as pl
from jax.experimental.pallas import tpu as pltpu
from jax.sharding import PartitionSpec as P

HD = 128
STRATA = 8
MESH = pl.DeviceIdType.MESH
NZ, NX, NY = 8, 4, 8
TOK = 256
COLS = 256
HALO = 16
EXT = TOK + HALO
KEYS = 640
NEG = -1e30

NT = (((1,), (1,)), ((), ()))
TN = (((0,), (0,)), ((), ()))
F32 = jnp.float32
BF16 = jnp.bfloat16


def dot(a, b, dims=(((1,), (0,)), ((), ()))):
    return lax.dot_general(a, b, dims, preferred_element_type=F32)


def kernel(
    q_hbm, k_hbm, v_hbm, g_hbm, w_hbm, len_ref, strata_ref, level_ref,
    dq_out, dk_out, dv_out, dw_out,
    q_all, k_all, v_all, g_all, gt, w_all, dacc, do_all, p_all, o_all, s_all,
    dq_all, dkv_own, o_ret, ret1, ret1_in, ret2, ret2_in, part, part_in,
    p_up, p_dn, zs, zr, red, xs, xr,
    local_sem, ag_send, ag_recv, sib_send, sib_recv, kv_send, kv_recv,
    ret_send, ret_recv, z_send, z_recv, x_send, x_recv,
):
    c = lax.axis_index("ctx")
    h = lax.axis_index("head")
    z, x, y, core = c // NX, c % NX, h // 2, h % 2
    side = c % 2
    sign = 2 * side - 1
    edge = pl.multiple_of(side * (TOK - HALO), HALO)

    def at_ctx(index):
        return {"ctx": (index + NZ * NX) % (NZ * NX), "head": h}

    def at_zx(zz, xx):
        return {"ctx": (zz + NZ) % NZ * NX + (xx + NX) % NX, "head": h}

    def at_y(yy):
        return {"ctx": c, "head": (yy + NY) % NY * 2 + core}

    y_up, y_dn = at_y(y + 1), at_y(y - 1)
    z_up, z_dn = at_zx(z + 1, x), at_zx(z - 1, x)
    x_up, x_dn = at_zx(z, x + 1), at_zx(z, x - 1)
    sibling = {"ctx": c, "head": h + 1 - 2 * core}
    partner = at_ctx(c - sign)
    mirror = at_ctx(c + sign)
    far_to, far_from = at_ctx(c + 2 * sign), at_ctx(c - 2 * sign)

    def remote(src, dst, ssem, rsem, device):
        return pltpu.make_async_remote_copy(
            src_ref=src, dst_ref=dst, send_sem=ssem, recv_sem=rsem, device_id=device, device_id_type=MESH
        )

    own = [
        pltpu.make_async_copy(src, dst, local_sem.at[n])
        for n, (src, dst) in enumerate(
            [
                (g_hbm, g_all.at[0, 0]),
                (q_hbm, q_all.at[pl.ds(0, TOK)]),
                (k_hbm, k_all.at[pl.ds(0, TOK)]),
                (v_hbm, v_all.at[pl.ds(0, TOK)]),
                (w_hbm, w_all),
            ]
        )
    ]
    for copy in own:
        copy.start()

    barrier = pltpu.get_barrier_semaphore()
    greeted = [y_up, y_dn, z_up, z_dn, x_up, x_dn, sibling, partner, mirror, far_to, far_from]
    for device in greeted:
        pl.semaphore_signal(barrier, inc=1, device_id=device, device_id_type=MESH)

    doc = c // 2
    position = c * TOK + lax.broadcasted_iota(jnp.int32, (1, TOK), 1)
    stratum = jnp.zeros((1, TOK), jnp.int32)
    begin = jnp.int32(0)
    doc_begin = jnp.int32(0)
    doc_end = jnp.int32(0)
    for n in range(16):
        finish = begin + len_ref[n]
        within = (position >= begin) & (position < finish)
        stratum = jnp.where(within, strata_ref[n], stratum)
        doc_begin = jnp.where(doc == n, begin, doc_begin)
        doc_end = jnp.where(doc == n, finish, doc_end)
        begin = finish
    level = level_ref[...].reshape(1, TOK)
    weight_row = jnp.where(level < stratum + 1, STRATA / (stratum + 1).astype(F32), 0.0)
    weight = jnp.transpose(jnp.broadcast_to(weight_row, (HD, TOK)))

    other = 1 - side

    def place(index, own_first, halo_first):
        return jnp.where(index < TOK, own_first + index, halo_first + index - TOK)

    own_first = c * TOK
    own_halo = own_first - HALO + (TOK + HALO) * side
    partner_first = (c - sign) * TOK
    partner_halo = partner_first - HALO + (TOK + HALO) * other
    rows = place(lax.broadcasted_iota(jnp.int32, (EXT, 1), 0), own_first, own_halo)
    row_in = ((rows >= doc_begin) & (rows < doc_end)).astype(F32)
    lane = lax.broadcasted_iota(jnp.int32, (1, KEYS), 1)
    keys_at = jnp.where(
        lane < TOK,
        own_first + lane,
        jnp.where(
            lane < 2 * TOK,
            partner_first + lane - TOK,
            jnp.where(lane < 2 * TOK + HALO, own_halo + lane - 2 * TOK, partner_halo + lane - 2 * TOK - HALO),
        ),
    )
    key_in = (keys_at >= doc_begin) & (keys_at < doc_end) & (lane < 2 * TOK + 2 * HALO)
    bias = jnp.where(key_in, 0.0, NEG)
    pad = KEYS - 2 * TOK - 2 * HALO
    k_all[pl.ds(KEYS - pad, pad), :] = jnp.zeros((pad, COLS), BF16)
    v_all[pl.ds(KEYS - pad, pad), :] = jnp.zeros((pad, COLS), BF16)

    pl.semaphore_wait(barrier, len(greeted))

    half = TOK // 2

    def ag_copy(up, s, part_index, from_own):
        rows_of = pl.ds(part_index * half, half)
        direction = 0 if up else 1
        slot_here = (NY - (s - 1)) % NY if up else s - 1
        slot_there = NY - s if up else s
        src = g_hbm.at[rows_of] if from_own else g_all.at[slot_here, 0, rows_of]
        index = direction * 8 + (s - 1) * 2 + part_index
        return remote(
            src, g_all.at[slot_there, 0, rows_of], ag_send.at[index], ag_recv.at[index], y_up if up else y_dn
        )

    def sib_copy(slot, part_index, from_own=False):
        rows_of = pl.ds(part_index * half, half)
        src = g_hbm.at[rows_of] if from_own else g_all.at[slot, 0, rows_of]
        index = slot * 2 + part_index
        return remote(src, g_all.at[slot, 1, rows_of], sib_send.at[index], sib_recv.at[index], sibling)

    ag = {}
    sib = {}
    for part_index in range(2):
        for up in (True, False):
            ag[up, 1, part_index] = ag_copy(up, 1, part_index, True)
            ag[up, 1, part_index].start()
    kv = [
        remote(k_hbm, k_all.at[pl.ds(TOK, TOK)], kv_send.at[0], kv_recv.at[0], partner),
        remote(v_hbm, v_all.at[pl.ds(TOK, TOK)], kv_send.at[1], kv_recv.at[1], partner),
    ]
    rim = pl.ds(edge, HALO)
    for n, (src, dst, device) in enumerate(
        [
            (k_hbm, k_all.at[pl.ds(2 * TOK, HALO)], mirror),
            (v_hbm, v_all.at[pl.ds(2 * TOK, HALO)], mirror),
            (q_hbm, q_all.at[pl.ds(TOK, HALO)], mirror),
            (k_hbm, k_all.at[pl.ds(2 * TOK + HALO, HALO)], far_to),
            (v_hbm, v_all.at[pl.ds(2 * TOK + HALO, HALO)], far_to),
        ]
    ):
        kv.append(remote(src.at[rim], dst, kv_send.at[2 + n], kv_recv.at[2 + n], device))
    for copy in kv[2:] + kv[:2]:
        copy.start()
    for part_index in range(2):
        sib[0, part_index] = sib_copy(0, part_index, True)
        sib[0, part_index].start()

    def take_block(slot, r):
        index = (y + slot) % NY * 2 + (core + r) % 2
        first = pl.multiple_of(index * COLS, COLS)
        block = g_all[slot, r]
        gt[pl.ds(first, COLS), :] = jnp.transpose(block)

    for copy in own:
        copy.wait()
    take_block(0, 0)
    for part_index in range(2):
        sib[0, part_index].wait_recv()
    take_block(0, 1)

    for s in range(1, NY // 2):
        for part_index in range(2):
            for up in (True, False):
                ag[up, s, part_index].wait_recv()
                if s + 1 < NY // 2 or part_index == (0 if up else 1):
                    ag[up, s + 1, part_index] = ag_copy(up, s + 1, part_index, False)
                    ag[up, s + 1, part_index].start()
                slot = NY - s if up else s
                sib[slot, part_index] = sib_copy(slot, part_index)
                sib[slot, part_index].start()
        for slot in (s, NY - s):
            take_block(slot, 0)
        if s > 1:
            for slot in (s - 1, NY - s + 1):
                for part_index in range(2):
                    sib[slot, part_index].wait_recv()
                take_block(slot, 1)

    scale = HD**-0.5
    for copy in kv:
        copy.wait_recv()
    for n in range(2):
        cols = pl.ds(n * HD, HD)
        scores = dot(q_all[:, cols], k_all[:, cols], NT) * scale + bias
        top = jnp.max(scores, axis=1, keepdims=True)
        terms = jnp.exp(scores - top)
        total = jnp.sum(terms, axis=1, keepdims=True)
        attention = terms * (row_in / total)
        p_all[n] = attention
        o_all[:, cols] = dot(attention.astype(BF16), v_all[:, cols])
    back = remote(o_all.at[pl.ds(TOK, HALO)], o_ret, ret_send.at[0], ret_recv.at[0], mirror)
    back.start()

    last = NY // 2
    for up in (True, False):
        part_index = 0 if up else 1
        ag[up, last, part_index].wait_recv()
        sib[last, part_index] = sib_copy(last, part_index)
        sib[last, part_index].start()
    for slot in (last - 1, last + 1):
        for part_index in range(2):
            sib[slot, part_index].wait_recv()
        take_block(slot, 1)
    take_block(last, 0)
    for part_index in range(2):
        sib[last, part_index].wait_recv()
    take_block(last, 1)

    back.wait_recv()
    s_all[...] = o_all[pl.ds(0, TOK), :]
    s_all[rim, :] += o_ret[...]
    for n in range(2):
        cols = pl.ds(n * HD, HD)
        s_all[:, cols] = s_all[:, cols] * weight
    scaled = s_all[...].astype(BF16)

    spots = [(x + 2) % NX, (x + 1) % NX, (x + NX - 1) % NX, x]
    DEST = 4096 // (NZ * NX)

    def z_block(zz):
        first = pl.multiple_of((zz + NZ) % NZ * (DEST * NX), DEST * NX)
        return dot(gt[pl.ds(first, DEST * NX), :], scaled)

    def rows_at(q):
        return pl.ds(pl.multiple_of(spots[q] * DEST, DEST), DEST)

    zc = {}

    def z_step(t):
        if t == 0:
            p_up[...] = z_block(z + 4)
        else:
            p_up[...] = z_block(z + 4 - t)
            p_dn[...] = z_block(z - 4 + t)
        for q in range(4):
            for up in (True, False):
                if t == 0 and (q < 2) != up:
                    continue
                source = p_up if up or t == 0 else p_dn
                value = source[rows_at(q), :]
                if (up, t - 1, q) in zc:
                    zc[up, t - 1, q].wait_recv()
                    value = value + zr[0 if up else 1, t - 1, q].astype(F32)
                d = 0 if up else 1
                zs[d, t, q] = value.astype(BF16)
                index = d * 16 + t * 4 + q
                zc[up, t, q] = remote(
                    zs.at[d, t, q], zr.at[d, t, q], z_send.at[index], z_recv.at[index], z_up if up else z_dn
                )
                zc[up, t, q].start()

    z_step(0)

    dacc[...] = jnp.zeros((TOK, COLS), F32)
    for slot in range(NY):
        for r in range(2):
            index = (y + slot) % NY * 2 + (core + r) % 2
            first = pl.multiple_of(index * COLS, COLS)
            dacc[...] += dot(g_all[slot, r], w_all[pl.ds(first, COLS), :])
    for n in range(2):
        cols = pl.ds(n * HD, HD)
        do_all[pl.ds(0, TOK), cols] = (dacc[:, cols] * weight).astype(BF16)
    halo_grad = remote(
        do_all.at[rim], do_all.at[pl.ds(TOK, HALO)], ret_send.at[1], ret_recv.at[1], mirror
    )
    halo_grad.start()

    z_step(1)

    halo_grad.wait_recv()

    def backward(n):
        cols = pl.ds(n * HD, HD)
        attention = p_all[n]
        grads = do_all[:, cols]
        correction = jnp.sum(grads.astype(F32) * o_all[:, cols], axis=1, keepdims=True)
        dots = dot(grads, v_all[:, cols], NT)
        score_grad = (attention * (dots - correction) * scale).astype(BF16)
        dq_all[:, cols] = dot(score_grad, k_all[:, cols])
        for which, value in enumerate(
            (dot(score_grad, q_all[:, cols], TN), dot(attention.astype(BF16), grads, TN))
        ):
            dkv_own[which, :, cols] = value[:TOK]
            part[which, :, cols] = value[TOK : 2 * TOK].astype(BF16)
            ret1[1 + which, :, cols] = value[2 * TOK : 2 * TOK + HALO]
            ret2[which, :, cols] = value[2 * TOK + HALO : 2 * TOK + 2 * HALO]

    backward(0)
    backward(1)
    ret1[0] = dq_all[pl.ds(TOK, HALO), :]
    returns = [
        remote(part, part_in, ret_send.at[2], ret_recv.at[2], partner),
        remote(ret1, ret1_in, ret_send.at[3], ret_recv.at[3], mirror),
        remote(ret2, ret2_in, ret_send.at[4], ret_recv.at[4], far_from),
    ]
    for copy in returns:
        copy.start()

    z_step(2)
    z_step(3)

    for copy in returns:
        copy.wait_recv()
    dq_all[rim, :] += ret1_in[0]
    dq_out[...] = dq_all[pl.ds(0, TOK), :].astype(BF16)
    for which, out in enumerate((dk_out, dv_out)):
        dkv_own[which, rim, :] += ret1_in[1 + which] + ret2_in[which]
        out[...] = (dkv_own[which] + part_in[which].astype(F32)).astype(BF16)

    p_up[...] = z_block(z)

    def z_sum(q):
        for up in (True, False):
            zc[up, 3, q].wait_recv()
        return p_up[rows_at(q), :] + zr[0, 3, q].astype(F32) + zr[1, 3, q].astype(F32)

    xc = []
    mid = DEST // 2
    red[0] = z_sum(0).astype(BF16)
    for n, (first, device) in enumerate(((0, x_up), (mid, x_dn))):
        here = pl.ds(first, mid)
        copy = remote(red.at[0, here], xr.at[n, here], x_send.at[n], x_recv.at[n], device)
        copy.start()
        xc.append(copy)
    for n, (first, device) in enumerate(((0, x_up), (mid, x_dn))):
        xs[...] = z_sum(1 + n)
        xc[n].wait_recv()
        here = pl.ds(first, mid)
        xs[here, :] += xr[n, here, :].astype(F32)
        red[1 + n] = xs[...].astype(BF16)
        copy = remote(red.at[1 + n], xr.at[2 + n], x_send.at[2 + n], x_recv.at[2 + n], device)
        copy.start()
        xc.append(copy)
    final = z_sum(3)
    for copy in xc[2:]:
        copy.wait_recv()
    dw_out[...] = final + xr[2].astype(F32) + xr[3].astype(F32)

    for copy in list(ag.values()) + list(sib.values()) + kv + [back, halo_grad] + returns + list(zc.values()) + xc:
        copy.wait_send()


def local(queries, keys, values, grad_out, out_weight, doc_lengths, strata, mask_level):
    hbm = pl.BlockSpec(memory_space=pl.ANY)
    smem = pl.BlockSpec(memory_space=pltpu.SMEM)
    vmem = pl.BlockSpec(memory_space=pltpu.VMEM)
    dma = pltpu.SemaphoreType.DMA
    V = pltpu.VMEM
    dest = 4096 // (NZ * NX)
    return pl.pallas_call(
        kernel,
        out_shape=[
            jax.ShapeDtypeStruct((TOK, COLS), BF16),
            jax.ShapeDtypeStruct((TOK, COLS), BF16),
            jax.ShapeDtypeStruct((TOK, COLS), BF16),
            jax.ShapeDtypeStruct((dest, COLS), F32),
        ],
        in_specs=[hbm] * 5 + [smem, smem, vmem],
        out_specs=[vmem] * 4,
        scratch_shapes=[
            V((EXT, COLS), BF16),
            V((KEYS, COLS), BF16),
            V((KEYS, COLS), BF16),
            V((NY, 2, TOK, COLS), BF16),
            V((4096, TOK), BF16),
            V((4096, COLS), BF16),
            V((TOK, COLS), F32),
            V((EXT, COLS), BF16),
            V((2, EXT, KEYS), F32),
            V((EXT, COLS), F32),
            V((TOK, COLS), F32),
            V((EXT, COLS), F32),
            V((2, TOK, COLS), F32),
            V((HALO, COLS), F32),
            V((3, HALO, COLS), F32),
            V((3, HALO, COLS), F32),
            V((2, HALO, COLS), F32),
            V((2, HALO, COLS), F32),
            V((2, TOK, COLS), BF16),
            V((2, TOK, COLS), BF16),
            V((dest * NX, COLS), F32),
            V((dest * NX, COLS), F32),
            V((2, 4, 4, dest, COLS), BF16),
            V((2, 4, 4, dest, COLS), BF16),
            V((3, dest, COLS), BF16),
            V((dest, COLS), F32),
            V((4, dest, COLS), BF16),
            dma((5,)),
            dma((16,)),
            dma((16,)),
            dma((16,)),
            dma((16,)),
            dma((7,)),
            dma((7,)),
            dma((5,)),
            dma((5,)),
            dma((32,)),
            dma((32,)),
            dma((4,)),
            dma((4,)),
        ],
        compiler_params=pltpu.CompilerParams(
            collective_id=0, has_side_effects=True, vmem_limit_bytes=56 * 2**20
        ),
    )(queries, keys, values, grad_out, out_weight, doc_lengths, strata, mask_level)


def solution(mesh):
    placed = (
        P("ctx", "head"),
        P("ctx", "head"),
        P("ctx", "head"),
        P("ctx", "head"),
        P(None, "head"),
        P(),
        P(),
        P("ctx"),
    )
    return jax.shard_map(
        local,
        mesh=mesh,
        in_specs=placed,
        out_specs=(P("ctx", "head"), P("ctx", "head"), P("ctx", "head"), P("ctx", "head")),
        check_vma=False,
    )
```

```python
import jax
import jax.numpy as jnp
from jax import lax
from jax.experimental import pallas as pl
from jax.experimental.pallas import tpu as pltpu
from jax.sharding import PartitionSpec as P

HD = 128
STRATA = 8
MESH = pl.DeviceIdType.MESH
NZ, NX, NY = 8, 4, 8
TOK = 256
COLS = 256
HALO = 16
EXT = TOK + HALO
KEYS = 640
NEG = -1e30
DEST = 4096 // (NZ * NX)
ROWS_Z = 64
ROWS_X = DEST - ROWS_Z

NT = (((1,), (1,)), ((), ()))
TN = (((0,), (0,)), ((), ()))
F32 = jnp.float32
BF16 = jnp.bfloat16


def dot(a, b, dims=(((1,), (0,)), ((), ()))):
    return lax.dot_general(a, b, dims, preferred_element_type=F32)


def kernel(
    q_hbm, k_hbm, v_hbm, g_hbm, w_hbm, len_hbm, strata_hbm, level_hbm,
    dq_out, dk_out, dv_out, dw_out,
    len_ref, strata_ref, level_ref,
    q_all, k_all, v_all, g_all, w_all, dacc, do_all, p_all, o_all, s_all,
    dq_all, dkv_own, o_ret, ret1, ret1_in, ret2, ret2_in, part, part_in,
    parts, zs, zr, xs0, xr0, xs1, xr1, z_out, z_in, x_out, x_in, total,
    local_sem, ag_send, ag_recv, sib_send, sib_recv, kv_send, kv_recv,
    ret_send, ret_recv, z_send, z_recv, x_send, x_recv, far_send, far_recv,
):
    c = lax.axis_index("ctx")
    h = lax.axis_index("head")
    z, x, y, core = c // NX, c % NX, h // 2, h % 2
    side = c % 2
    sign = 2 * side - 1
    edge = pl.multiple_of(side * (TOK - HALO), HALO)

    def at_ctx(index):
        return {"ctx": (index + NZ * NX) % (NZ * NX), "head": h}

    def at_zx(zz, xx):
        return {"ctx": (zz + NZ) % NZ * NX + (xx + NX) % NX, "head": h}

    def at_y(yy):
        return {"ctx": c, "head": (yy + NY) % NY * 2 + core}

    y_up, y_dn = at_y(y + 1), at_y(y - 1)
    z_up, z_dn = at_zx(z + 1, x), at_zx(z - 1, x)
    x_up, x_dn = at_zx(z, x + 1), at_zx(z, x - 1)
    sibling = {"ctx": c, "head": h + 1 - 2 * core}
    partner = at_ctx(c - sign)
    mirror = at_ctx(c + sign)
    far_to, far_from = at_ctx(c + 2 * sign), at_ctx(c - 2 * sign)

    def remote(src, dst, ssem, rsem, device):
        return pltpu.make_async_remote_copy(
            src_ref=src, dst_ref=dst, send_sem=ssem, recv_sem=rsem, device_id=device, device_id_type=MESH
        )

    barrier = pltpu.get_barrier_semaphore()
    greeted = [y_up, y_dn, sibling, partner, mirror, far_to, far_from]
    greeted += [at_zx(z, x + d) for d in range(1, NX)] + [at_zx(z + d, x) for d in range(1, NZ)]
    for device in greeted:
        pl.semaphore_signal(barrier, inc=1, device_id=device, device_id_type=MESH)

    own = [
        pltpu.make_async_copy(src, dst, local_sem.at[n])
        for n, (src, dst) in enumerate(
            [
                (len_hbm, len_ref),
                (strata_hbm, strata_ref),
                (level_hbm, level_ref),
                (g_hbm, g_all.at[0, 0]),
                (q_hbm, q_all.at[pl.ds(0, TOK)]),
                (k_hbm, k_all.at[pl.ds(0, TOK)]),
                (v_hbm, v_all.at[pl.ds(0, TOK)]),
                (w_hbm, w_all),
            ]
        )
    ]
    for copy in own:
        copy.start()

    pl.semaphore_wait(barrier, len(greeted))

    half = TOK // 2

    def ag_copy(up, s, part_index, from_own):
        rows_of = pl.ds(part_index * half, half)
        direction = 0 if up else 1
        slot_here = (NY - (s - 1)) % NY if up else s - 1
        slot_there = NY - s if up else s
        src = g_hbm.at[rows_of] if from_own else g_all.at[slot_here, 0, rows_of]
        index = direction * 8 + (s - 1) * 2 + part_index
        return remote(
            src, g_all.at[slot_there, 0, rows_of], ag_send.at[index], ag_recv.at[index], y_up if up else y_dn
        )

    def sib_copy(slot):
        return remote(
            g_all.at[slot, 0] if slot else g_hbm, g_all.at[slot, 1], sib_send.at[slot], sib_recv.at[slot], sibling
        )

    ag = {}
    sib = {}
    for part_index in range(2):
        for up in (True, False):
            ag[up, 1, part_index] = ag_copy(up, 1, part_index, True)
            ag[up, 1, part_index].start()
    kv = [
        remote(k_hbm, k_all.at[pl.ds(TOK, TOK)], kv_send.at[0], kv_recv.at[0], partner),
        remote(v_hbm, v_all.at[pl.ds(TOK, TOK)], kv_send.at[1], kv_recv.at[1], partner),
    ]
    rim = pl.ds(edge, HALO)
    for n, (src, dst, device) in enumerate(
        [
            (k_hbm, k_all.at[pl.ds(2 * TOK, HALO)], mirror),
            (v_hbm, v_all.at[pl.ds(2 * TOK, HALO)], mirror),
            (q_hbm, q_all.at[pl.ds(TOK, HALO)], mirror),
            (k_hbm, k_all.at[pl.ds(2 * TOK + HALO, HALO)], far_to),
            (v_hbm, v_all.at[pl.ds(2 * TOK + HALO, HALO)], far_to),
        ]
    ):
        kv.append(remote(src.at[rim], dst, kv_send.at[2 + n], kv_recv.at[2 + n], device))
    for copy in kv[2:] + kv[:2]:
        copy.start()
    def pass_on(slot):
        sib[slot] = sib_copy(slot)
        sib[slot].start()

    pass_on(0)

    for copy in own:
        copy.wait()

    doc = c // 2
    position = c * TOK + lax.broadcasted_iota(jnp.int32, (1, TOK), 1)
    stratum = jnp.zeros((1, TOK), jnp.int32)
    begin = jnp.int32(0)
    doc_begin = jnp.int32(0)
    doc_end = jnp.int32(0)
    for n in range(16):
        finish = begin + len_ref[n]
        within = (position >= begin) & (position < finish)
        stratum = jnp.where(within, strata_ref[n], stratum)
        doc_begin = jnp.where(doc == n, begin, doc_begin)
        doc_end = jnp.where(doc == n, finish, doc_end)
        begin = finish
    level = level_ref[...].reshape(1, TOK)
    weight_row = jnp.where(level < stratum + 1, STRATA / (stratum + 1).astype(F32), 0.0)
    weight = jnp.transpose(jnp.broadcast_to(weight_row, (HD, TOK)))

    other = 1 - side

    def place(index, own_first, halo_first):
        return jnp.where(index < TOK, own_first + index, halo_first + index - TOK)

    own_first = c * TOK
    own_halo = own_first - HALO + (TOK + HALO) * side
    partner_first = (c - sign) * TOK
    partner_halo = partner_first - HALO + (TOK + HALO) * other
    rows = place(lax.broadcasted_iota(jnp.int32, (EXT, 1), 0), own_first, own_halo)
    row_in = ((rows >= doc_begin) & (rows < doc_end)).astype(F32)
    lane = lax.broadcasted_iota(jnp.int32, (1, KEYS), 1)
    keys_at = jnp.where(
        lane < TOK,
        own_first + lane,
        jnp.where(
            lane < 2 * TOK,
            partner_first + lane - TOK,
            jnp.where(lane < 2 * TOK + HALO, own_halo + lane - 2 * TOK, partner_halo + lane - 2 * TOK - HALO),
        ),
    )
    key_in = (keys_at >= doc_begin) & (keys_at < doc_end) & (lane < 2 * TOK + 2 * HALO)
    bias = jnp.where(key_in, 0.0, NEG)
    pad = KEYS - 2 * TOK - 2 * HALO
    k_all[pl.ds(KEYS - pad, pad), :] = jnp.zeros((pad, COLS), BF16)
    v_all[pl.ds(KEYS - pad, pad), :] = jnp.zeros((pad, COLS), BF16)

    def ag_step(s):
        for part_index in range(2):
            for up in (True, False):
                ag[up, s, part_index].wait_recv()
                if s + 1 < NY // 2 or part_index == (0 if up else 1):
                    ag[up, s + 1, part_index] = ag_copy(up, s + 1, part_index, False)
                    ag[up, s + 1, part_index].start()
        pass_on(NY - s)
        pass_on(s)

    ag_step(1)
    ag_step(2)

    scale = HD**-0.5
    for copy in kv:
        copy.wait_recv()

    def forward(n, first, count):
        rows_of, cols = pl.ds(first, count), pl.ds(n * HD, HD)
        scores = dot(q_all[rows_of, cols], k_all[:, cols], NT) * scale + bias
        top = jnp.max(scores, axis=1, keepdims=True)
        terms = jnp.exp(scores - top)
        attention = terms * (row_in[first : first + count] / jnp.sum(terms, axis=1, keepdims=True))
        p_all[n, rows_of, :] = attention
        o_all[rows_of, cols] = dot(attention.astype(BF16), v_all[:, cols])

    forward(0, TOK, HALO)
    forward(1, TOK, HALO)
    back = remote(o_all.at[pl.ds(TOK, HALO)], o_ret, ret_send.at[0], ret_recv.at[0], mirror)
    back.start()
    forward(0, 0, TOK)
    forward(1, 0, TOK)

    ag_step(3)

    back.wait_recv()
    s_all[...] = o_all[pl.ds(0, TOK), :]
    s_all[rim, :] += o_ret[...]
    for n in range(2):
        cols = pl.ds(n * HD, HD)
        s_all[:, cols] = s_all[:, cols] * weight
    scaled = s_all[...].astype(BF16)

    spots = [(x + 2) % NX, (x + 1) % NX, (x + NX - 1) % NX, x]

    def make_part(d):
        if d:
            sib[d].wait_recv()
        for r in range(2):
            first = (y + d) % NY * (2 * COLS) + (core + r) % 2 * COLS
            parts[pl.ds(pl.multiple_of(first, COLS), COLS), :] = dot(g_all[d, r], scaled, TN)

    def part_z(e, q):
        first = (z + e) % NZ * (NX * DEST) + spots[q] * DEST
        return parts[pl.ds(pl.multiple_of(first, DEST), ROWS_Z), :]

    def part_x(d, q):
        first = (y + d) % NY * (NX * DEST) + spots[q] * DEST + ROWS_Z
        return parts[pl.ds(pl.multiple_of(first, 16), ROWS_X), :]

    zc = {}

    def z_send_slot(up, t, q):
        e = 4 - t if up else (4 + t) % NZ
        value = part_z(e, q)
        d = 0 if up else 1
        if (up, t - 1, q) in zc:
            zc[up, t - 1, q].wait_recv()
            value = value + zr[d, t - 1, q].astype(F32)
        zs[d, t, q] = value.astype(BF16)
        index = d * 16 + t * 4 + q
        zc[up, t, q] = remote(
            zs.at[d, t, q], zr.at[d, t, q], z_send.at[index], z_recv.at[index], z_up if up else z_dn
        )
        zc[up, t, q].start()

    def z_first(t):
        for q in range(2):
            z_send_slot(True, t, q)
            z_send_slot(False, t, q + 2)

    def z_second(t):
        for q in range(2):
            z_send_slot(True, t, q + 2)
            z_send_slot(False, t, q)

    xc = {}
    pairs = ((0, 1), (7, 2), (6, 3), (5, 4))

    def x_start(u):
        for n, up in enumerate((True, False)):
            xs0[u, n] = part_x(pairs[u][n], 0).astype(BF16)
            index = u * 2 + n
            xc[up, 0, u] = remote(
                xs0.at[u, n], xr0.at[u, n], x_send.at[index], x_recv.at[index], x_up if up else x_dn
            )
            xc[up, 0, u].start()

    def x_next(u):
        for n, up in enumerate((True, False)):
            for m in range(2):
                value = part_x(pairs[u][m], 1 if up else 2)
                if m == n:
                    xc[up, 0, u].wait_recv()
                    value = value + xr0[u, n].astype(F32)
                xs1[u, n, m] = value.astype(BF16)
            index = 8 + u * 2 + n
            xc[up, 1, u] = remote(
                xs1.at[u, n], xr1.at[u, n], x_send.at[index], x_recv.at[index], x_up if up else x_dn
            )
            xc[up, 1, u].start()

    straight = []

    def to_z(d):
        e = (y + d - z + NZ) % NZ
        return e, remote(z_out.at[d], z_in.at[e], far_send.at[d], far_recv.at[e], at_zx(y + d, x))

    def to_z_in(e):
        return remote(z_out.at[0], z_in.at[e], far_send.at[0], far_recv.at[e], at_zx(z + e, x))

    def x_total(u):
        for up in (True, False):
            xc[up, 1, u].wait_recv()
        for m, d in enumerate(pairs[u]):
            value = part_x(d, 3) + xr1[u, 0, m].astype(F32) + xr1[u, 1, m].astype(F32)
            z_out[d] = value.astype(BF16)
            e, copy = to_z(d)

            @pl.when(e != 0)
            def _():
                copy.start()

            @pl.when(e == 0)
            def _():
                total[pl.ds(ROWS_Z, ROWS_X), :] = value

    sib[0].wait_recv()
    for d in (0, 1, 7, 2):
        make_part(d)
    x_start(0)
    x_start(1)
    for d in (6, 3):
        make_part(d)
    x_start(2)
    last = NY // 2
    for up in (True, False):
        ag[up, last, 0 if up else 1].wait_recv()
    pass_on(last)
    x_next(0)
    x_next(1)
    make_part(5)
    make_part(4)
    z_first(0)
    x_start(3)
    z_second(1)

    dacc[...] = jnp.zeros((TOK, COLS), F32)
    for slot in range(NY):
        for r in range(2):
            index = (y + slot) % NY * 2 + (core + r) % 2
            first = pl.multiple_of(index * COLS, COLS)
            dacc[...] += dot(g_all[slot, r], w_all[pl.ds(first, COLS), :])
    for n in range(2):
        cols = pl.ds(n * HD, HD)
        do_all[pl.ds(0, TOK), cols] = (dacc[:, cols] * weight).astype(BF16)
    halo_grad = remote(
        do_all.at[rim], do_all.at[pl.ds(TOK, HALO)], ret_send.at[1], ret_recv.at[1], mirror
    )
    halo_grad.start()

    z_first(1)
    x_next(2)
    z_second(2)
    x_next(3)

    halo_grad.wait_recv()

    def backward(n):
        cols = pl.ds(n * HD, HD)
        attention = p_all[n]
        grads = do_all[:, cols]
        correction = jnp.sum(grads.astype(F32) * o_all[:, cols], axis=1, keepdims=True)
        dots = dot(grads, v_all[:, cols], NT)
        score_grad = (attention * (dots - correction) * scale).astype(BF16)
        dq_all[:, cols] = dot(score_grad, k_all[:, cols])
        for which, value in enumerate(
            (dot(score_grad, q_all[:, cols], TN), dot(attention.astype(BF16), grads, TN))
        ):
            dkv_own[which, :, cols] = value[:TOK]
            part[which, :, cols] = value[TOK : 2 * TOK].astype(BF16)
            ret1[1 + which, :, cols] = value[2 * TOK : 2 * TOK + HALO]
            ret2[which, :, cols] = value[2 * TOK + HALO : 2 * TOK + 2 * HALO]

    x_total(0)
    x_total(1)
    backward(0)
    z_first(2)
    backward(1)
    ret1[0] = dq_all[pl.ds(TOK, HALO), :]
    returns = [
        remote(part, part_in, ret_send.at[2], ret_recv.at[2], partner),
        remote(ret1, ret1_in, ret_send.at[3], ret_recv.at[3], mirror),
        remote(ret2, ret2_in, ret_send.at[4], ret_recv.at[4], far_from),
    ]
    for copy in returns:
        copy.start()

    z_second(3)
    x_total(2)
    x_total(3)
    z_first(3)

    def z_total(q):
        for up in (True, False):
            zc[up, 3, q].wait_recv()
        return part_z(0, q) + zr[0, 3, q].astype(F32) + zr[1, 3, q].astype(F32)

    for copy in returns:
        copy.wait_recv()
    dq_all[rim, :] += ret1_in[0]
    dq_out[...] = dq_all[pl.ds(0, TOK), :].astype(BF16)
    for which, out in enumerate((dk_out, dv_out)):
        dkv_own[which, rim, :] += ret1_in[1 + which] + ret2_in[which]
        out[...] = (dkv_own[which] + part_in[which].astype(F32)).astype(BF16)

    for q, d in ((0, 2), (1, 1), (2, NX - 1)):
        x_out[q] = z_total(q).astype(BF16)
        copy = remote(x_out.at[q], x_in.at[q], far_send.at[NZ + q], far_recv.at[NZ + q], at_zx(z, x + d))
        copy.start()
        straight.append(copy)
    total[pl.ds(0, ROWS_Z), :] = z_total(3)
    for e in range(1, NZ):
        to_z_in(e).wait_recv()
    for copy in straight:
        copy.wait_recv()
    for q in range(3):
        total[pl.ds(0, ROWS_Z), :] += x_in[q].astype(F32)
    for e in range(1, NZ):
        total[pl.ds(ROWS_Z, ROWS_X), :] += z_in[e].astype(F32)
    dw_out[...] = total[...]

    for copy in list(ag.values()) + list(sib.values()) + kv + [back, halo_grad] + returns + list(zc.values()):
        copy.wait_send()
    for copy in list(xc.values()) + straight:
        copy.wait_send()
    for d in range(NZ):
        e, copy = to_z(d)

        @pl.when(e != 0)
        def _(copy=copy):
            copy.wait_send()


def tail(*refs):
    count = len(refs) // 2
    sems = refs[-1]
    copies = [pltpu.make_async_copy(refs[n], refs[count + n], sems.at[n]) for n in range(count)]
    for copy in copies:
        copy.start()
    for copy in copies:
        copy.wait()


def local(queries, keys, values, grad_out, out_weight, doc_lengths, strata, mask_level):
    hbm = pl.BlockSpec(memory_space=pl.ANY)
    vmem = pl.BlockSpec(memory_space=pltpu.VMEM)
    dma = pltpu.SemaphoreType.DMA
    V = pltpu.VMEM
    outs = pl.pallas_call(
        kernel,
        out_shape=[
            V((TOK, COLS), BF16),
            V((TOK, COLS), BF16),
            V((TOK, COLS), BF16),
            V((DEST, COLS), F32),
        ],
        in_specs=[hbm] * 8,
        out_specs=[vmem] * 4,
        scratch_shapes=[
            pltpu.SMEM((16,), jnp.int32),
            pltpu.SMEM((16,), jnp.int32),
            V((TOK,), jnp.int32),
            V((EXT, COLS), BF16),
            V((KEYS, COLS), BF16),
            V((KEYS, COLS), BF16),
            V((NY, 2, TOK, COLS), BF16),
            V((4096, COLS), BF16),
            V((TOK, COLS), F32),
            V((EXT, COLS), BF16),
            V((2, EXT, KEYS), F32),
            V((EXT, COLS), F32),
            V((TOK, COLS), F32),
            V((EXT, COLS), F32),
            V((2, TOK, COLS), F32),
            V((HALO, COLS), F32),
            V((3, HALO, COLS), F32),
            V((3, HALO, COLS), F32),
            V((2, HALO, COLS), F32),
            V((2, HALO, COLS), F32),
            V((2, TOK, COLS), BF16),
            V((2, TOK, COLS), BF16),
            V((NZ * NX * DEST, COLS), F32),
            V((2, 4, 4, ROWS_Z, COLS), BF16),
            V((2, 4, 4, ROWS_Z, COLS), BF16),
            V((4, 2, ROWS_X, COLS), BF16),
            V((4, 2, ROWS_X, COLS), BF16),
            V((4, 2, 2, ROWS_X, COLS), BF16),
            V((4, 2, 2, ROWS_X, COLS), BF16),
            V((NZ, ROWS_X, COLS), BF16),
            V((NZ, ROWS_X, COLS), BF16),
            V((3, ROWS_Z, COLS), BF16),
            V((3, ROWS_Z, COLS), BF16),
            V((DEST, COLS), F32),
            dma((8,)),
            dma((16,)),
            dma((16,)),
            dma((8,)),
            dma((8,)),
            dma((7,)),
            dma((7,)),
            dma((5,)),
            dma((5,)),
            dma((32,)),
            dma((32,)),
            dma((16,)),
            dma((16,)),
            dma((NZ + 3,)),
            dma((NZ + 3,)),
        ],
        compiler_params=pltpu.CompilerParams(
            collective_id=0, has_side_effects=True, vmem_limit_bytes=60 * 2**20
        ),
    )(queries, keys, values, grad_out, out_weight, doc_lengths, strata, mask_level)
    return pl.pallas_call(
        tail,
        out_shape=[jax.ShapeDtypeStruct(a.shape, a.dtype) for a in outs],
        in_specs=[vmem] * 4,
        out_specs=[hbm] * 4,
        scratch_shapes=[dma((4,))],
        compiler_params=pltpu.CompilerParams(vmem_limit_bytes=8 * 2**20),
    )(*outs)


def solution(mesh):
    placed = (
        P("ctx", "head"),
        P("ctx", "head"),
        P("ctx", "head"),
        P("ctx", "head"),
        P(None, "head"),
        P(),
        P(),
        P("ctx"),
    )
    return jax.shard_map(
        local,
        mesh=mesh,
        in_specs=placed,
        out_specs=(P("ctx", "head"), P("ctx", "head"), P("ctx", "head"), P("ctx", "head")),
        check_vma=False,
    )
```

```python
import jax
import jax.numpy as jnp
from jax import lax
from jax.experimental import pallas as pl
from jax.experimental.pallas import tpu as pltpu
from jax.sharding import PartitionSpec as P

HD = 128
STRATA = 8
MESH = pl.DeviceIdType.MESH
NZ, NX, NY = 8, 4, 8
TOK = 256
COLS = 256
HALO = 16
EXT = TOK + HALO
KEYS = 640
NEG = -1e30
DEST = 4096 // (NZ * NX)
ROWS_Z = 64
ROWS_X = DEST - ROWS_Z

NT = (((1,), (1,)), ((), ()))
TN = (((0,), (0,)), ((), ()))
F32 = jnp.float32
BF16 = jnp.bfloat16


def dot(a, b, dims=(((1,), (0,)), ((), ()))):
    return lax.dot_general(a, b, dims, preferred_element_type=F32)


def kernel(
    q_hbm, k_hbm, v_hbm, g_hbm, w_hbm, len_hbm, strata_hbm, level_hbm,
    dq_out, dk_out, dv_out, dw_out,
    len_ref, strata_ref, level_ref,
    q_all, k_all, v_all, g_all, w_all, dacc, do_all, p_all, o_all, s_all,
    dq_all, dkv_own, o_ret, ret1, ret1_in, ret2, ret2_in, part, part_in,
    parts, zs, zr, xs0, xr0, xs1, xr1, totals, z_sum, z_out, z_in, x_out, x_in, total,
    local_sem, ag_send, ag_recv, sib_send, sib_recv, kv_send, kv_recv,
    ret_send, ret_recv, z_send, z_recv, x_send, x_recv, far_send, far_recv,
):
    c = lax.axis_index("ctx")
    h = lax.axis_index("head")
    z, x, y, core = c // NX, c % NX, h // 2, h % 2
    side = c % 2
    sign = 2 * side - 1
    edge = pl.multiple_of(side * (TOK - HALO), HALO)

    def at_ctx(index):
        return {"ctx": (index + NZ * NX) % (NZ * NX), "head": h}

    def at_zx(zz, xx):
        return {"ctx": (zz + NZ) % NZ * NX + (xx + NX) % NX, "head": h}

    def at_y(yy, k):
        return {"ctx": c, "head": (yy + NY) % NY * 2 + k}

    z_up, z_dn = at_zx(z + 1, x), at_zx(z - 1, x)
    x_up, x_dn = at_zx(z, x + 1), at_zx(z, x - 1)
    sibling = {"ctx": c, "head": h + 1 - 2 * core}
    partner = at_ctx(c - sign)
    mirror = at_ctx(c + sign)
    far_to, far_from = at_ctx(c + 2 * sign), at_ctx(c - 2 * sign)

    def remote(src, dst, ssem, rsem, device):
        return pltpu.make_async_remote_copy(
            src_ref=src, dst_ref=dst, send_sem=ssem, recv_sem=rsem, device_id=device, device_id_type=MESH
        )

    barrier = pltpu.get_barrier_semaphore()
    greeted = [at_y(y + d, k) for d in (1, -1) for k in range(2)] + [sibling, partner, mirror, far_to, far_from]
    greeted += [at_zx(z, x + d) for d in range(1, NX)] + [at_zx(z + d, x) for d in range(1, NZ)]
    for device in greeted:
        pl.semaphore_signal(barrier, inc=1, device_id=device, device_id_type=MESH)

    own = [
        pltpu.make_async_copy(src, dst, local_sem.at[n])
        for n, (src, dst) in enumerate(
            [
                (len_hbm, len_ref),
                (strata_hbm, strata_ref),
                (level_hbm, level_ref),
                (g_hbm, g_all.at[0, core]),
                (q_hbm, q_all.at[pl.ds(0, TOK)]),
                (k_hbm, k_all.at[pl.ds(0, TOK)]),
                (v_hbm, v_all.at[pl.ds(0, TOK)]),
                (w_hbm, w_all),
            ]
        )
    ]
    for copy in own:
        copy.start()

    pl.semaphore_wait(barrier, len(greeted))

    chunk = TOK // 4

    def chunk_at(p, k):
        return pl.ds(pl.multiple_of((p + 2 * k) % 4 * chunk, chunk), chunk)

    ag = []

    def ag_first(p, up):
        rows_of = chunk_at(p, 0 if up else 1)
        copy = remote(
            g_hbm.at[rows_of], g_all.at[NY - 1 if up else 1, core, rows_of],
            ag_send.at[p if up else 4 + p], ag_recv.at[core * 4 + p],
            at_y(y + 1, 0) if up else at_y(y - 1, 1),
        )
        copy.start()
        ag.append(copy)

    onward = at_y(y + 1 - 2 * core, core)

    def slot_at(s):
        return (NY + (2 * core - 1) * s) % NY

    def ag_copy(s, k, p):
        rows_of = chunk_at(p, core)
        index = 8 * s + 4 * k + p
        return remote(
            g_all.at[slot_at(s), k, rows_of], g_all.at[slot_at(s + 1), k, rows_of],
            ag_send.at[index], ag_recv.at[index], onward,
        )

    def ag_arrival(s, k, p):
        rows_of = chunk_at(p, core)
        index = 8 * (s - 1) + 4 * k + p
        here = g_all.at[slot_at(s), k, rows_of]
        remote(here, here, ag_send.at[index], ag_recv.at[index], onward).wait_recv()

    for p in range(4):
        for up in (True, False):
            ag_first(p, up)
    kv = [
        remote(k_hbm, k_all.at[pl.ds(TOK, TOK)], kv_send.at[0], kv_recv.at[0], partner),
        remote(v_hbm, v_all.at[pl.ds(TOK, TOK)], kv_send.at[1], kv_recv.at[1], partner),
    ]
    rim = pl.ds(edge, HALO)
    for n, (src, dst, device) in enumerate(
        [
            (k_hbm, k_all.at[pl.ds(2 * TOK, HALO)], mirror),
            (v_hbm, v_all.at[pl.ds(2 * TOK, HALO)], mirror),
            (q_hbm, q_all.at[pl.ds(TOK, HALO)], mirror),
            (k_hbm, k_all.at[pl.ds(2 * TOK + HALO, HALO)], far_to),
            (v_hbm, v_all.at[pl.ds(2 * TOK + HALO, HALO)], far_to),
        ]
    ):
        kv.append(remote(src.at[rim], dst, kv_send.at[2 + n], kv_recv.at[2 + n], device))
    for copy in kv[2:] + kv[:2]:
        copy.start()
    sib = []

    def pass_on(s):
        if s == 0:
            src, dst = g_hbm, g_all.at[0, core]
        elif s < NY // 2:
            src = dst = g_all.at[slot_at(s)]
        else:
            src = dst = g_all.at[s, :, pl.ds(pl.multiple_of(core * (TOK // 2), TOK // 2), TOK // 2)]
        copy = remote(src, dst, sib_send.at[s], sib_recv.at[s], sibling)
        copy.start()
        sib.append(copy)

    def from_sibling(s):
        if s == 0:
            here = g_all.at[0, 1 - core]
        elif s < NY // 2:
            here = g_all.at[slot_at(-s)]
        else:
            here = g_all.at[s, :, pl.ds(pl.multiple_of((1 - core) * (TOK // 2), TOK // 2), TOK // 2)]
        remote(here, here, sib_send.at[s], sib_recv.at[s], sibling).wait_recv()

    pass_on(0)

    for copy in own:
        copy.wait()

    doc = c // 2
    position = c * TOK + lax.broadcasted_iota(jnp.int32, (1, TOK), 1)
    stratum = jnp.zeros((1, TOK), jnp.int32)
    begin = jnp.int32(0)
    doc_begin = jnp.int32(0)
    doc_end = jnp.int32(0)
    for n in range(16):
        finish = begin + len_ref[n]
        within = (position >= begin) & (position < finish)
        stratum = jnp.where(within, strata_ref[n], stratum)
        doc_begin = jnp.where(doc == n, begin, doc_begin)
        doc_end = jnp.where(doc == n, finish, doc_end)
        begin = finish
    level = level_ref[...].reshape(1, TOK)
    weight_row = jnp.where(level < stratum + 1, STRATA / (stratum + 1).astype(F32), 0.0)
    weight = jnp.transpose(jnp.broadcast_to(weight_row, (HD, TOK)))

    other = 1 - side

    def place(index, own_first, halo_first):
        return jnp.where(index < TOK, own_first + index, halo_first + index - TOK)

    own_first = c * TOK
    own_halo = own_first - HALO + (TOK + HALO) * side
    partner_first = (c - sign) * TOK
    partner_halo = partner_first - HALO + (TOK + HALO) * other
    rows = place(lax.broadcasted_iota(jnp.int32, (EXT, 1), 0), own_first, own_halo)
    row_in = ((rows >= doc_begin) & (rows < doc_end)).astype(F32)
    lane = lax.broadcasted_iota(jnp.int32, (1, KEYS), 1)
    keys_at = jnp.where(
        lane < TOK,
        own_first + lane,
        jnp.where(
            lane < 2 * TOK,
            partner_first + lane - TOK,
            jnp.where(lane < 2 * TOK + HALO, own_halo + lane - 2 * TOK, partner_halo + lane - 2 * TOK - HALO),
        ),
    )
    key_in = (keys_at >= doc_begin) & (keys_at < doc_end) & (lane < 2 * TOK + 2 * HALO)
    bias = jnp.where(key_in, 0.0, NEG)
    pad = KEYS - 2 * TOK - 2 * HALO
    k_all[pl.ds(KEYS - pad, pad), :] = jnp.zeros((pad, COLS), BF16)
    v_all[pl.ds(KEYS - pad, pad), :] = jnp.zeros((pad, COLS), BF16)

    def ag_step(s):
        for p in range(4 if s < NY // 2 else 2):
            for k in range(2):
                ag_arrival(s, k, p)
                if s < NY // 2 and (s + 1 < NY // 2 or p < 2):
                    copy = ag_copy(s, k, p)
                    copy.start()
                    ag.append(copy)
        pass_on(s)

    ag_step(1)
    ag_step(2)

    scale = HD**-0.5
    for copy in kv:
        copy.wait_recv()

    def forward(n, first, count):
        rows_of, cols = pl.ds(first, count), pl.ds(n * HD, HD)
        scores = dot(q_all[rows_of, cols], k_all[:, cols], NT) * scale + bias
        top = jnp.max(scores, axis=1, keepdims=True)
        terms = jnp.exp(scores - top)
        attention = terms * (row_in[first : first + count] / jnp.sum(terms, axis=1, keepdims=True))
        p_all[n, rows_of, :] = attention
        o_all[rows_of, cols] = dot(attention.astype(BF16), v_all[:, cols])

    forward(0, TOK, HALO)
    forward(1, TOK, HALO)
    back = remote(o_all.at[pl.ds(TOK, HALO)], o_ret, ret_send.at[0], ret_recv.at[0], mirror)
    back.start()
    forward(0, 0, TOK)
    forward(1, 0, TOK)

    ag_step(3)

    back.wait_recv()
    s_all[...] = o_all[pl.ds(0, TOK), :]
    s_all[rim, :] += o_ret[...]
    for n in range(2):
        cols = pl.ds(n * HD, HD)
        s_all[:, cols] = s_all[:, cols] * weight
    scaled = s_all[...].astype(BF16)

    spots = [(x + 2) % NX, (x + 1) % NX, (x + NX - 1) % NX, x]

    def make_part(d):
        for r in range(2):
            first = (y + d) % NY * (2 * COLS) + r * COLS
            parts[pl.ds(pl.multiple_of(first, COLS), COLS), :] = dot(g_all[d, r], scaled, TN)

    def part_z(e, q):
        first = (z + e) % NZ * (NX * DEST) + spots[q] * DEST
        return parts[pl.ds(pl.multiple_of(first, DEST), ROWS_Z), :]

    def part_x(d, q):
        first = (y + d) % NY * (NX * DEST) + spots[q] * DEST + ROWS_Z
        return parts[pl.ds(pl.multiple_of(first, 16), ROWS_X), :]

    zc = {}

    def z_send_group(up, t, late):
        e = 4 - t if up else (4 + t) % NZ
        d, group = 0 if up else 1, 0 if up != late else 1
        came = zc.get((up, t - 1, late))
        if came is not None:
            came.wait_recv()
        for n in range(2):
            value = part_z(e, group * 2 + n)
            if came is not None:
                value = value + zr[d, t - 1, group, n].astype(F32)
            zs[d, t, group, n] = value.astype(BF16)
        index = d * 8 + t * 2 + group
        copy = remote(
            zs.at[d, t, group], zr.at[d, t, group], z_send.at[index], z_recv.at[index], z_up if up else z_dn
        )
        copy.start()
        zc[up, t, late] = copy

    def z_first(t):
        z_send_group(True, t, False)
        z_send_group(False, t, False)

    def z_second(t):
        z_send_group(True, t, True)
        z_send_group(False, t, True)

    xc = {}
    pairs = ((0, 1), (7, 2), (6, 3), (5, 4))

    def x_start(u):
        for n, up in enumerate((True, False)):
            xs0[u, n] = part_x(pairs[u][n], 0).astype(BF16)
            index = u * 2 + n
            xc[up, 0, u] = remote(
                xs0.at[u, n], xr0.at[u, n], x_send.at[index], x_recv.at[index], x_up if up else x_dn
            )
            xc[up, 0, u].start()

    def x_next(u):
        for n, up in enumerate((True, False)):
            for m in range(2):
                value = part_x(pairs[u][m], 1 if up else 2)
                if m == n:
                    xc[up, 0, u].wait_recv()
                    value = value + xr0[u, n].astype(F32)
                xs1[u, n, m] = value.astype(BF16)
            index = 8 + u * 2 + n
            xc[up, 1, u] = remote(
                xs1.at[u, n], xr1.at[u, n], x_send.at[index], x_recv.at[index], x_up if up else x_dn
            )
            xc[up, 1, u].start()

    def x_total(u):
        for up in (True, False):
            xc[up, 1, u].wait_recv()
        for m, d in enumerate(pairs[u]):
            totals[(y + d) % NY] = part_x(d, 3) + xr1[u, 0, m].astype(F32) + xr1[u, 1, m].astype(F32)

    straight = []

    def over_z(n, e, first, count, hop, *more):
        value = totals[(z + e) % NZ, first : first + count]
        for slot in more:
            straight[slot].wait_recv()
            if slot < 2:
                here = slice(0, ROWS_X // 2) if slot == 0 else slice(ROWS_X // 2, ROWS_X)
                z_sum[...] = value
                z_sum[here] += z_in[slot, : ROWS_X // 2].astype(F32)
                value = z_sum[...]
            else:
                value = value + z_in[slot].astype(F32)
        z_out[n, :count] = value.astype(BF16)
        here = pl.ds(0, count)
        copy = remote(
            z_out.at[n, here], z_in.at[n, here], far_send.at[n], far_recv.at[n], at_zx(z + hop, x)
        )
        copy.start()
        straight.append(copy)

    for s in range(3):
        from_sibling(s)
    for d in (0, 1, 7, 2):
        make_part(d)
    x_start(0)
    x_start(1)
    ag_step(NY // 2)
    from_sibling(3)
    for d in (6, 3):
        make_part(d)
    x_start(2)
    make_part(5)

    def grad_block(slot):
        value = None
        for r in range(2):
            first = (y + slot) % NY * (2 * COLS) + r * COLS
            term = dot(g_all[slot, r], w_all[pl.ds(pl.multiple_of(first, COLS), COLS), :])
            value = term if value is None else value + term
        return value

    dacc[...] = grad_block(0)
    for slot in (1, 7, 2, 6, 3, 5):
        dacc[...] += grad_block(slot)

    from_sibling(NY // 2)
    make_part(4)
    z_first(0)
    x_start(3)
    z_second(1)

    dacc[...] += grad_block(4)
    for n in range(2):
        cols = pl.ds(n * HD, HD)
        do_all[pl.ds(0, TOK), cols] = (dacc[:, cols] * weight).astype(BF16)
    halo_grad = remote(
        do_all.at[rim], do_all.at[pl.ds(TOK, HALO)], ret_send.at[1], ret_recv.at[1], mirror
    )
    halo_grad.start()

    x_next(0)
    x_next(1)
    z_first(1)
    x_next(2)
    z_second(2)
    x_next(3)

    halo_grad.wait_recv()

    def backward(n):
        cols = pl.ds(n * HD, HD)
        attention = p_all[n]
        grads = do_all[:, cols]
        correction = jnp.sum(grads.astype(F32) * o_all[:, cols], axis=1, keepdims=True)
        dots = dot(grads, v_all[:, cols], NT)
        score_grad = (attention * (dots - correction) * scale).astype(BF16)
        dq_all[:, cols] = dot(score_grad, k_all[:, cols])
        for which, value in enumerate(
            (dot(score_grad, q_all[:, cols], TN), dot(attention.astype(BF16), grads, TN))
        ):
            dkv_own[which, :, cols] = value[:TOK]
            part[which, :, cols] = value[TOK : 2 * TOK].astype(BF16)
            ret1[1 + which, :, cols] = value[2 * TOK : 2 * TOK + HALO]
            ret2[which, :, cols] = value[2 * TOK + HALO : 2 * TOK + 2 * HALO]

    backward(0)
    z_first(2)
    backward(1)
    ret1[0] = dq_all[pl.ds(TOK, HALO), :]
    returns = [
        remote(part, part_in, ret_send.at[2], ret_recv.at[2], partner),
        remote(ret1, ret1_in, ret_send.at[3], ret_recv.at[3], mirror),
        remote(ret2, ret2_in, ret_send.at[4], ret_recv.at[4], far_from),
    ]
    for copy in returns:
        copy.start()

    z_second(3)
    for u in range(4):
        x_total(u)
    mid = ROWS_X // 2
    over_z(0, 4, 0, mid, 2)
    over_z(1, 4, mid, mid, -2)
    over_z(2, 3, 0, ROWS_X, 1)
    over_z(3, 5, 0, ROWS_X, -1)
    over_z(4, 1, 0, ROWS_X, 1)
    over_z(5, 7, 0, ROWS_X, -1)
    z_first(3)
    over_z(6, 2, 0, ROWS_X, 2, 0, 2)
    over_z(7, 6, 0, ROWS_X, -2, 1, 3)
    total[pl.ds(ROWS_Z, ROWS_X), :] = totals[z]

    def z_total(q):
        value = part_z(0, q)
        for d, up in ((0, True), (1, False)):
            late = (q >= 2) == up
            if (d, q // 2) not in arrived:
                zc[up, 3, late].wait_recv()
                arrived.add((d, q // 2))
            value = value + zr[d, 3, q // 2, q % 2].astype(F32)
        return value

    arrived = set()
    for q, d in ((0, 2), (1, 1), (2, NX - 1)):
        x_out[q] = z_total(q).astype(BF16)
        copy = remote(x_out.at[q], x_in.at[q], far_send.at[NZ + q], far_recv.at[NZ + q], at_zx(z, x + d))
        copy.start()
        straight.append(copy)
    total[pl.ds(0, ROWS_Z), :] = z_total(3)

    for copy in returns:
        copy.wait_recv()
    dq_all[rim, :] += ret1_in[0]
    dq_out[...] = dq_all[pl.ds(0, TOK), :].astype(BF16)
    for which, out in enumerate((dk_out, dv_out)):
        dkv_own[which, rim, :] += ret1_in[1 + which] + ret2_in[which]
        out[...] = (dkv_own[which] + part_in[which].astype(F32)).astype(BF16)

    for copy in straight[4:]:
        copy.wait_recv()
    for n in range(4, NZ):
        total[pl.ds(ROWS_Z, ROWS_X), :] += z_in[n].astype(F32)
    for q in range(3):
        total[pl.ds(0, ROWS_Z), :] += x_in[q].astype(F32)
    dw_out[...] = total[...]

    for copy in ag + sib + kv + [back, halo_grad] + returns + list(zc.values()):
        copy.wait_send()
    for copy in list(xc.values()) + straight:
        copy.wait_send()


def tail(*refs):
    count = len(refs) // 2
    sems = refs[-1]
    copies = [pltpu.make_async_copy(refs[n], refs[count + n], sems.at[n]) for n in range(count)]
    for copy in copies:
        copy.start()
    for copy in copies:
        copy.wait()


def local(queries, keys, values, grad_out, out_weight, doc_lengths, strata, mask_level):
    hbm = pl.BlockSpec(memory_space=pl.ANY)
    vmem = pl.BlockSpec(memory_space=pltpu.VMEM)
    dma = pltpu.SemaphoreType.DMA
    V = pltpu.VMEM
    outs = pl.pallas_call(
        kernel,
        out_shape=[
            V((TOK, COLS), BF16),
            V((TOK, COLS), BF16),
            V((TOK, COLS), BF16),
            V((DEST, COLS), F32),
        ],
        in_specs=[hbm] * 8,
        out_specs=[vmem] * 4,
        scratch_shapes=[
            pltpu.SMEM((16,), jnp.int32),
            pltpu.SMEM((16,), jnp.int32),
            V((TOK,), jnp.int32),
            V((EXT, COLS), BF16),
            V((KEYS, COLS), BF16),
            V((KEYS, COLS), BF16),
            V((NY, 2, TOK, COLS), BF16),
            V((4096, COLS), BF16),
            V((TOK, COLS), F32),
            V((EXT, COLS), BF16),
            V((2, EXT, KEYS), F32),
            V((EXT, COLS), F32),
            V((TOK, COLS), F32),
            V((EXT, COLS), F32),
            V((2, TOK, COLS), F32),
            V((HALO, COLS), F32),
            V((3, HALO, COLS), F32),
            V((3, HALO, COLS), F32),
            V((2, HALO, COLS), F32),
            V((2, HALO, COLS), F32),
            V((2, TOK, COLS), BF16),
            V((2, TOK, COLS), BF16),
            V((NZ * NX * DEST, COLS), F32),
            V((2, 4, 2, 2, ROWS_Z, COLS), BF16),
            V((2, 4, 2, 2, ROWS_Z, COLS), BF16),
            V((4, 2, ROWS_X, COLS), BF16),
            V((4, 2, ROWS_X, COLS), BF16),
            V((4, 2, 2, ROWS_X, COLS), BF16),
            V((4, 2, 2, ROWS_X, COLS), BF16),
            V((NZ, ROWS_X, COLS), F32),
            V((ROWS_X, COLS), F32),
            V((NZ, ROWS_X, COLS), BF16),
            V((NZ, ROWS_X, COLS), BF16),
            V((3, ROWS_Z, COLS), BF16),
            V((3, ROWS_Z, COLS), BF16),
            V((DEST, COLS), F32),
            dma((8,)),
            dma((32,)),
            dma((32,)),
            dma((5,)),
            dma((5,)),
            dma((7,)),
            dma((7,)),
            dma((5,)),
            dma((5,)),
            dma((16,)),
            dma((16,)),
            dma((16,)),
            dma((16,)),
            dma((NZ + 3,)),
            dma((NZ + 3,)),
        ],
        compiler_params=pltpu.CompilerParams(
            collective_id=0, has_side_effects=True, vmem_limit_bytes=60 * 2**20
        ),
    )(queries, keys, values, grad_out, out_weight, doc_lengths, strata, mask_level)
    return pl.pallas_call(
        tail,
        out_shape=[jax.ShapeDtypeStruct(a.shape, a.dtype) for a in outs],
        in_specs=[vmem] * 4,
        out_specs=[hbm] * 4,
        scratch_shapes=[dma((4,))],
        compiler_params=pltpu.CompilerParams(vmem_limit_bytes=8 * 2**20),
    )(*outs)


def solution(mesh):
    placed = (
        P("ctx", "head"),
        P("ctx", "head"),
        P("ctx", "head"),
        P("ctx", "head"),
        P(None, "head"),
        P(),
        P(),
        P("ctx"),
    )
    return jax.shard_map(
        local,
        mesh=mesh,
        in_specs=placed,
        out_specs=(P("ctx", "head"), P("ctx", "head"), P("ctx", "head"), P("ctx", "head")),
        check_vma=False,
    )
```

```python
import jax
import jax.numpy as jnp
from jax import lax
from jax.experimental import pallas as pl
from jax.experimental.pallas import tpu as pltpu
from jax.sharding import PartitionSpec as P

HD = 128
STRATA = 8
MESH = pl.DeviceIdType.MESH
NZ, NX, NY = 8, 4, 8
TOK = 256
COLS = 256
HALO = 16
EXT = TOK + HALO
KEYS = 640
NEG = -1e30
DEST = 4096 // (NZ * NX)
ROWS_Z = 64
ROWS_X = DEST - ROWS_Z

NT = (((1,), (1,)), ((), ()))
TN = (((0,), (0,)), ((), ()))
F32 = jnp.float32
BF16 = jnp.bfloat16


def dot(a, b, dims=(((1,), (0,)), ((), ()))):
    return lax.dot_general(a, b, dims, preferred_element_type=F32)


def kernel(
    q_hbm, k_hbm, v_hbm, g_hbm, w_hbm, len_hbm, strata_hbm, level_hbm,
    dq_out, dk_out, dv_out, dw_out,
    len_ref, strata_ref, level_ref,
    q_all, k_all, v_all, g_all, w_all, dacc, do_all, p_all, o_all, s_all,
    dq_all, dkv_own, o_ret, ret1, ret1_in, ret2, ret2_in, part, part_in,
    parts, zs, zr, xs0, xr0, xs1, xr1, totals, z_sum, z_out, z_in, x_out, x_in, total,
    local_sem, ag_send, ag_recv, sib_send, sib_recv, kv_send, kv_recv,
    ret_send, ret_recv, z_send, z_recv, x_send, x_recv, far_send, far_recv,
):
    c = lax.axis_index("ctx")
    h = lax.axis_index("head")
    z, x, y, core = c // NX, c % NX, h // 2, h % 2
    side = c % 2
    sign = 2 * side - 1
    edge = pl.multiple_of(side * (TOK - HALO), HALO)

    def at_ctx(index):
        return {"ctx": (index + NZ * NX) % (NZ * NX), "head": h}

    def at_zx(zz, xx):
        return {"ctx": (zz + NZ) % NZ * NX + (xx + NX) % NX, "head": h}

    def at_y(yy, k):
        return {"ctx": c, "head": (yy + NY) % NY * 2 + k}

    z_up, z_dn = at_zx(z + 1, x), at_zx(z - 1, x)
    x_up, x_dn = at_zx(z, x + 1), at_zx(z, x - 1)
    sibling = {"ctx": c, "head": h + 1 - 2 * core}
    partner = at_ctx(c - sign)
    mirror = at_ctx(c + sign)
    far_to, far_from = at_ctx(c + 2 * sign), at_ctx(c - 2 * sign)

    def remote(src, dst, ssem, rsem, device):
        return pltpu.make_async_remote_copy(
            src_ref=src, dst_ref=dst, send_sem=ssem, recv_sem=rsem, device_id=device, device_id_type=MESH
        )

    barrier = pltpu.get_barrier_semaphore()
    greeted = [at_y(y + d, k) for d in (1, -1) for k in range(2)] + [sibling, partner, mirror, far_to, far_from]
    greeted += [at_zx(z, x + d) for d in range(1, NX)] + [at_zx(z + d, x) for d in (1, 2, -2, -1)]
    for device in greeted:
        pl.semaphore_signal(barrier, inc=1, device_id=device, device_id_type=MESH)

    own = [
        pltpu.make_async_copy(src, dst, local_sem.at[n])
        for n, (src, dst) in enumerate(
            [
                (len_hbm, len_ref),
                (strata_hbm, strata_ref),
                (level_hbm, level_ref),
                (g_hbm, g_all.at[0, core]),
                (q_hbm, q_all.at[pl.ds(0, TOK)]),
                (k_hbm, k_all.at[pl.ds(0, TOK)]),
                (v_hbm, v_all.at[pl.ds(0, TOK)]),
                (w_hbm, w_all),
            ]
        )
    ]
    for copy in own:
        copy.start()

    pl.semaphore_wait(barrier, len(greeted))

    chunk = TOK // 4

    def chunk_at(p, k):
        return pl.ds(pl.multiple_of((p + 2 * k) % 4 * chunk, chunk), chunk)

    ag = []

    def ag_first(p, up):
        rows_of = chunk_at(p, 0 if up else 1)
        copy = remote(
            g_hbm.at[rows_of], g_all.at[NY - 1 if up else 1, core, rows_of],
            ag_send.at[p if up else 4 + p], ag_recv.at[core * 4 + p],
            at_y(y + 1, 0) if up else at_y(y - 1, 1),
        )
        copy.start()
        ag.append(copy)

    onward = at_y(y + 1 - 2 * core, core)

    def slot_at(s):
        return (NY + (2 * core - 1) * s) % NY

    def ag_copy(s, k, p):
        rows_of = chunk_at(p, core)
        index = 8 * s + 4 * k + p
        return remote(
            g_all.at[slot_at(s), k, rows_of], g_all.at[slot_at(s + 1), k, rows_of],
            ag_send.at[index], ag_recv.at[index], onward,
        )

    def ag_arrival(s, k, p):
        rows_of = chunk_at(p, core)
        index = 8 * (s - 1) + 4 * k + p
        here = g_all.at[slot_at(s), k, rows_of]
        remote(here, here, ag_send.at[index], ag_recv.at[index], onward).wait_recv()

    for p in range(4):
        for up in (True, False):
            ag_first(p, up)
    kv = [
        remote(k_hbm, k_all.at[pl.ds(TOK, TOK)], kv_send.at[0], kv_recv.at[0], partner),
        remote(v_hbm, v_all.at[pl.ds(TOK, TOK)], kv_send.at[1], kv_recv.at[1], partner),
    ]
    rim = pl.ds(edge, HALO)
    for n, (src, dst, device) in enumerate(
        [
            (k_hbm, k_all.at[pl.ds(2 * TOK, HALO)], mirror),
            (v_hbm, v_all.at[pl.ds(2 * TOK, HALO)], mirror),
            (q_hbm, q_all.at[pl.ds(TOK, HALO)], mirror),
            (k_hbm, k_all.at[pl.ds(2 * TOK + HALO, HALO)], far_to),
            (v_hbm, v_all.at[pl.ds(2 * TOK + HALO, HALO)], far_to),
        ]
    ):
        kv.append(remote(src.at[rim], dst, kv_send.at[2 + n], kv_recv.at[2 + n], device))
    for copy in kv[2:] + kv[:2]:
        copy.start()
    sib = []

    def pass_on(s):
        if s == 0:
            src, dst = g_hbm, g_all.at[0, core]
        elif s < NY // 2:
            src = dst = g_all.at[slot_at(s)]
        else:
            src = dst = g_all.at[s, :, pl.ds(pl.multiple_of(core * (TOK // 2), TOK // 2), TOK // 2)]
        copy = remote(src, dst, sib_send.at[s], sib_recv.at[s], sibling)
        copy.start()
        sib.append(copy)

    def from_sibling(s):
        if s == 0:
            here = g_all.at[0, 1 - core]
        elif s < NY // 2:
            here = g_all.at[slot_at(-s)]
        else:
            here = g_all.at[s, :, pl.ds(pl.multiple_of((1 - core) * (TOK // 2), TOK // 2), TOK // 2)]
        remote(here, here, sib_send.at[s], sib_recv.at[s], sibling).wait_recv()

    pass_on(0)

    for copy in own:
        copy.wait()

    doc = c // 2
    position = c * TOK + lax.broadcasted_iota(jnp.int32, (1, TOK), 1)
    stratum = jnp.zeros((1, TOK), jnp.int32)
    begin = jnp.int32(0)
    doc_begin = jnp.int32(0)
    doc_end = jnp.int32(0)
    for n in range(16):
        finish = begin + len_ref[n]
        within = (position >= begin) & (position < finish)
        stratum = jnp.where(within, strata_ref[n], stratum)
        doc_begin = jnp.where(doc == n, begin, doc_begin)
        doc_end = jnp.where(doc == n, finish, doc_end)
        begin = finish
    level = level_ref[...].reshape(1, TOK)
    weight_row = jnp.where(level < stratum + 1, STRATA / (stratum + 1).astype(F32), 0.0)
    weight = jnp.transpose(jnp.broadcast_to(weight_row, (HD, TOK)))

    other = 1 - side

    def place(index, own_first, halo_first):
        return jnp.where(index < TOK, own_first + index, halo_first + index - TOK)

    own_first = c * TOK
    own_halo = own_first - HALO + (TOK + HALO) * side
    partner_first = (c - sign) * TOK
    partner_halo = partner_first - HALO + (TOK + HALO) * other
    rows = place(lax.broadcasted_iota(jnp.int32, (EXT, 1), 0), own_first, own_halo)
    row_in = ((rows >= doc_begin) & (rows < doc_end)).astype(F32)
    lane = lax.broadcasted_iota(jnp.int32, (1, KEYS), 1)
    keys_at = jnp.where(
        lane < TOK,
        own_first + lane,
        jnp.where(
            lane < 2 * TOK,
            partner_first + lane - TOK,
            jnp.where(lane < 2 * TOK + HALO, own_halo + lane - 2 * TOK, partner_halo + lane - 2 * TOK - HALO),
        ),
    )
    key_in = (keys_at >= doc_begin) & (keys_at < doc_end) & (lane < 2 * TOK + 2 * HALO)
    bias = jnp.where(key_in, 0.0, NEG)
    pad = KEYS - 2 * TOK - 2 * HALO
    k_all[pl.ds(KEYS - pad, pad), :] = jnp.zeros((pad, COLS), BF16)
    v_all[pl.ds(KEYS - pad, pad), :] = jnp.zeros((pad, COLS), BF16)

    def ag_step(s, between=None):
        for p in range(4 if s < NY // 2 else 2):
            if p == 2 and between is not None:
                between()
            for k in range(2):
                ag_arrival(s, k, p)
                if s < NY // 2 and (s + 1 < NY // 2 or p < 2):
                    copy = ag_copy(s, k, p)
                    copy.start()
                    ag.append(copy)
        pass_on(s)

    ag_step(1)
    ag_step(2)

    scale = HD**-0.5
    for copy in kv:
        copy.wait_recv()

    def forward(n, first, count):
        rows_of, cols = pl.ds(first, count), pl.ds(n * HD, HD)
        scores = dot(q_all[rows_of, cols], k_all[:, cols], NT) * scale + bias
        top = jnp.max(scores, axis=1, keepdims=True)
        terms = jnp.exp(scores - top)
        attention = terms * (row_in[first : first + count] / jnp.sum(terms, axis=1, keepdims=True))
        p_all[n, rows_of, :] = attention
        o_all[rows_of, cols] = dot(attention.astype(BF16), v_all[:, cols])

    forward(0, TOK, HALO)
    forward(1, TOK, HALO)
    back = remote(o_all.at[pl.ds(TOK, HALO)], o_ret, ret_send.at[0], ret_recv.at[0], mirror)
    back.start()
    forward(0, 0, TOK)
    forward(1, 0, TOK)

    ag_step(3)
    ag_step(NY // 2)

    back.wait_recv()
    s_all[...] = o_all[pl.ds(0, TOK), :]
    s_all[rim, :] += o_ret[...]
    for n in range(2):
        cols = pl.ds(n * HD, HD)
        s_all[:, cols] = s_all[:, cols] * weight
    scaled = s_all[...].astype(BF16)

    spots = [(x + 2) % NX, (x + 1) % NX, (x + NX - 1) % NX, x]

    def make_part(d):
        for r in range(2):
            first = (y + d) % NY * (2 * COLS) + r * COLS
            parts[pl.ds(pl.multiple_of(first, COLS), COLS), :] = dot(g_all[d, r], scaled, TN)

    def part_z(e, q):
        first = (z + e) % NZ * (NX * DEST) + spots[q] * DEST
        return parts[pl.ds(pl.multiple_of(first, DEST), ROWS_Z), :]

    def part_x(d, q):
        first = (y + d) % NY * (NX * DEST) + spots[q] * DEST + ROWS_Z
        return parts[pl.ds(pl.multiple_of(first, 16), ROWS_X), :]

    zc = {}

    def z_send_group(up, t, late):
        e = 4 - t if up else (4 + t) % NZ
        d, group = 0 if up else 1, 0 if up != late else 1
        came = zc.get((up, t - 1, late))
        if came is not None:
            came.wait_recv()
        for n in range(2):
            value = part_z(e, group * 2 + n)
            if came is not None:
                value = value + zr[d, t - 1, group, n].astype(F32)
            zs[d, t, group, n] = value.astype(BF16)
        index = d * 8 + t * 2 + group
        copy = remote(
            zs.at[d, t, group], zr.at[d, t, group], z_send.at[index], z_recv.at[index], z_up if up else z_dn
        )
        copy.start()
        zc[up, t, late] = copy

    def z_first(t):
        z_send_group(True, t, False)
        z_send_group(False, t, False)

    def z_second(t):
        z_send_group(True, t, True)
        z_send_group(False, t, True)

    xc = {}
    pairs = ((0, 1), (7, 2), (6, 3), (5, 4))

    def x_start(u):
        for n, up in enumerate((True, False)):
            xs0[u, n] = part_x(pairs[u][n], 0).astype(BF16)
            index = u * 2 + n
            xc[up, 0, u] = remote(
                xs0.at[u, n], xr0.at[u, n], x_send.at[index], x_recv.at[index], x_up if up else x_dn
            )
            xc[up, 0, u].start()

    def x_next(u):
        for n, up in enumerate((True, False)):
            for m in range(2):
                value = part_x(pairs[u][m], 1 if up else 2)
                if m == n:
                    xc[up, 0, u].wait_recv()
                    value = value + xr0[u, n].astype(F32)
                xs1[u, n, m] = value.astype(BF16)
            index = 8 + u * 2 + n
            xc[up, 1, u] = remote(
                xs1.at[u, n], xr1.at[u, n], x_send.at[index], x_recv.at[index], x_up if up else x_dn
            )
            xc[up, 1, u].start()

    def x_total(u):
        for up in (True, False):
            xc[up, 1, u].wait_recv()
        for m, d in enumerate(pairs[u]):
            totals[(y + d) % NY] = part_x(d, 3) + xr1[u, 0, m].astype(F32) + xr1[u, 1, m].astype(F32)

    straight = []

    def over_z(n, e, first, count, hop, *more):
        value = totals[(z + e) % NZ, first : first + count]
        for slot in more:
            straight[slot].wait_recv()
            if slot < 2:
                here = slice(0, ROWS_X // 2) if slot == 0 else slice(ROWS_X // 2, ROWS_X)
                z_sum[...] = value
                z_sum[here] += z_in[slot, : ROWS_X // 2].astype(F32)
                value = z_sum[...]
            else:
                value = value + z_in[slot].astype(F32)
        z_out[n, :count] = value.astype(BF16)
        here = pl.ds(0, count)
        copy = remote(
            z_out.at[n, here], z_in.at[n, here], far_send.at[n], far_recv.at[n], at_zx(z + hop, x)
        )
        copy.start()
        straight.append(copy)

    for s in range(3):
        from_sibling(s)
    for d in (0, 1, 7, 2):
        make_part(d)
    x_start(0)
    x_start(1)
    from_sibling(3)
    for d in (6, 3):
        make_part(d)
    x_start(2)
    make_part(5)

    def grad_block(slot):
        value = None
        for r in range(2):
            first = (y + slot) % NY * (2 * COLS) + r * COLS
            term = dot(g_all[slot, r], w_all[pl.ds(pl.multiple_of(first, COLS), COLS), :])
            value = term if value is None else value + term
        return value

    dacc[...] = grad_block(0)
    for slot in (1, 7, 2, 6, 3, 5):
        dacc[...] += grad_block(slot)

    from_sibling(NY // 2)
    make_part(4)
    z_first(0)
    x_start(3)
    z_second(1)

    dacc[...] += grad_block(4)
    for n in range(2):
        cols = pl.ds(n * HD, HD)
        do_all[pl.ds(0, TOK), cols] = (dacc[:, cols] * weight).astype(BF16)
    halo_grad = remote(
        do_all.at[rim], do_all.at[pl.ds(TOK, HALO)], ret_send.at[1], ret_recv.at[1], mirror
    )
    halo_grad.start()

    x_next(0)
    x_next(1)
    z_first(1)
    x_next(2)
    z_second(2)
    x_next(3)

    halo_grad.wait_recv()

    def backward(n):
        cols = pl.ds(n * HD, HD)
        attention = p_all[n]
        grads = do_all[:, cols]
        correction = jnp.sum(grads.astype(F32) * o_all[:, cols], axis=1, keepdims=True)
        dots = dot(grads, v_all[:, cols], NT)
        score_grad = (attention * (dots - correction) * scale).astype(BF16)
        dq_all[:, cols] = dot(score_grad, k_all[:, cols])
        for which, value in enumerate(
            (dot(score_grad, q_all[:, cols], TN), dot(attention.astype(BF16), grads, TN))
        ):
            dkv_own[which, :, cols] = value[:TOK]
            part[which, :, cols] = value[TOK : 2 * TOK].astype(BF16)
            ret1[1 + which, :, cols] = value[2 * TOK : 2 * TOK + HALO]
            ret2[which, :, cols] = value[2 * TOK + HALO : 2 * TOK + 2 * HALO]

    backward(0)
    z_first(2)
    backward(1)
    ret1[0] = dq_all[pl.ds(TOK, HALO), :]
    returns = [
        remote(part, part_in, ret_send.at[2], ret_recv.at[2], partner),
        remote(ret1, ret1_in, ret_send.at[3], ret_recv.at[3], mirror),
        remote(ret2, ret2_in, ret_send.at[4], ret_recv.at[4], far_from),
    ]
    for copy in returns:
        copy.start()

    z_second(3)
    for u in range(4):
        x_total(u)
    mid = ROWS_X // 2
    over_z(0, 4, 0, mid, 2)
    over_z(1, 4, mid, mid, -2)
    over_z(2, 3, 0, ROWS_X, 1)
    over_z(3, 5, 0, ROWS_X, -1)
    z_first(3)
    over_z(4, 1, 0, ROWS_X, 1)
    over_z(5, 7, 0, ROWS_X, -1)
    over_z(6, 2, 0, ROWS_X, 2, 0, 2)
    over_z(7, 6, 0, ROWS_X, -2, 1, 3)
    total[pl.ds(ROWS_Z, ROWS_X), :] = totals[z]

    def z_total(q):
        value = part_z(0, q)
        for d, up in ((0, True), (1, False)):
            late = (q >= 2) == up
            if (d, q // 2) not in arrived:
                zc[up, 3, late].wait_recv()
                arrived.add((d, q // 2))
            value = value + zr[d, 3, q // 2, q % 2].astype(F32)
        return value

    arrived = set()
    for q, d in ((0, 2), (1, 1), (2, NX - 1)):
        x_out[q] = z_total(q).astype(BF16)
        copy = remote(x_out.at[q], x_in.at[q], far_send.at[NZ + q], far_recv.at[NZ + q], at_zx(z, x + d))
        copy.start()
        straight.append(copy)
    total[pl.ds(0, ROWS_Z), :] = z_total(3)

    for copy in returns:
        copy.wait_recv()
    dq_all[rim, :] += ret1_in[0]
    dq_out[...] = dq_all[pl.ds(0, TOK), :].astype(BF16)
    for which, out in enumerate((dk_out, dv_out)):
        dkv_own[which, rim, :] += ret1_in[1 + which] + ret2_in[which]
        out[...] = (dkv_own[which] + part_in[which].astype(F32)).astype(BF16)

    for copy in straight[4:]:
        copy.wait_recv()
    for n in range(4, NZ):
        total[pl.ds(ROWS_Z, ROWS_X), :] += z_in[n].astype(F32)
    for q in range(3):
        total[pl.ds(0, ROWS_Z), :] += x_in[q].astype(F32)
    dw_out[...] = total[...]

    for copy in ag + sib + kv + [back, halo_grad] + returns + list(zc.values()):
        copy.wait_send()
    for copy in list(xc.values()) + straight:
        copy.wait_send()


def tail(*refs):
    count = len(refs) // 2
    sems = refs[-1]
    copies = [pltpu.make_async_copy(refs[n], refs[count + n], sems.at[n]) for n in range(count)]
    for copy in copies:
        copy.start()
    for copy in copies:
        copy.wait()


def local(queries, keys, values, grad_out, out_weight, doc_lengths, strata, mask_level):
    hbm = pl.BlockSpec(memory_space=pl.ANY)
    vmem = pl.BlockSpec(memory_space=pltpu.VMEM)
    dma = pltpu.SemaphoreType.DMA
    V = pltpu.VMEM
    outs = pl.pallas_call(
        kernel,
        out_shape=[
            V((TOK, COLS), BF16),
            V((TOK, COLS), BF16),
            V((TOK, COLS), BF16),
            V((DEST, COLS), F32),
        ],
        in_specs=[hbm] * 8,
        out_specs=[vmem] * 4,
        scratch_shapes=[
            pltpu.SMEM((16,), jnp.int32),
            pltpu.SMEM((16,), jnp.int32),
            V((TOK,), jnp.int32),
            V((EXT, COLS), BF16),
            V((KEYS, COLS), BF16),
            V((KEYS, COLS), BF16),
            V((NY, 2, TOK, COLS), BF16),
            V((4096, COLS), BF16),
            V((TOK, COLS), F32),
            V((EXT, COLS), BF16),
            V((2, EXT, KEYS), F32),
            V((EXT, COLS), F32),
            V((TOK, COLS), F32),
            V((EXT, COLS), F32),
            V((2, TOK, COLS), F32),
            V((HALO, COLS), F32),
            V((3, HALO, COLS), F32),
            V((3, HALO, COLS), F32),
            V((2, HALO, COLS), F32),
            V((2, HALO, COLS), F32),
            V((2, TOK, COLS), BF16),
            V((2, TOK, COLS), BF16),
            V((NZ * NX * DEST, COLS), F32),
            V((2, 4, 2, 2, ROWS_Z, COLS), BF16),
            V((2, 4, 2, 2, ROWS_Z, COLS), BF16),
            V((4, 2, ROWS_X, COLS), BF16),
            V((4, 2, ROWS_X, COLS), BF16),
            V((4, 2, 2, ROWS_X, COLS), BF16),
            V((4, 2, 2, ROWS_X, COLS), BF16),
            V((NZ, ROWS_X, COLS), F32),
            V((ROWS_X, COLS), F32),
            V((NZ, ROWS_X, COLS), BF16),
            V((NZ, ROWS_X, COLS), BF16),
            V((3, ROWS_Z, COLS), BF16),
            V((3, ROWS_Z, COLS), BF16),
            V((DEST, COLS), F32),
            dma((8,)),
            dma((32,)),
            dma((32,)),
            dma((5,)),
            dma((5,)),
            dma((7,)),
            dma((7,)),
            dma((5,)),
            dma((5,)),
            dma((16,)),
            dma((16,)),
            dma((16,)),
            dma((16,)),
            dma((NZ + 3,)),
            dma((NZ + 3,)),
        ],
        compiler_params=pltpu.CompilerParams(
            collective_id=0, has_side_effects=True, vmem_limit_bytes=60 * 2**20
        ),
    )(queries, keys, values, grad_out, out_weight, doc_lengths, strata, mask_level)
    return pl.pallas_call(
        tail,
        out_shape=[jax.ShapeDtypeStruct(a.shape, a.dtype) for a in outs],
        in_specs=[vmem] * 4,
        out_specs=[hbm] * 4,
        scratch_shapes=[dma((4,))],
        compiler_params=pltpu.CompilerParams(vmem_limit_bytes=8 * 2**20),
    )(*outs)


def solution(mesh):
    placed = (
        P("ctx", "head"),
        P("ctx", "head"),
        P("ctx", "head"),
        P("ctx", "head"),
        P(None, "head"),
        P(),
        P(),
        P("ctx"),
    )
    return jax.shard_map(
        local,
        mesh=mesh,
        in_specs=placed,
        out_specs=(P("ctx", "head"), P("ctx", "head"), P("ctx", "head"), P("ctx", "head")),
        check_vma=False,
    )
```

```python
import jax
import jax.numpy as jnp
from jax import lax
from jax.experimental import pallas as pl
from jax.experimental.pallas import tpu as pltpu
from jax.sharding import PartitionSpec as P

HD = 128
STRATA = 8
MESH = pl.DeviceIdType.MESH
NZ, NX, NY = 8, 4, 8
TOK = 256
COLS = 256
HALO = 16
EXT = TOK + HALO
KEYS = 640
NEG = -1e30
DEST = 4096 // (NZ * NX)
ROWS_Z = 64
ROWS_X = DEST - ROWS_Z

NT = (((1,), (1,)), ((), ()))
TN = (((0,), (0,)), ((), ()))
F32 = jnp.float32
BF16 = jnp.bfloat16


def dot(a, b, dims=(((1,), (0,)), ((), ()))):
    return lax.dot_general(a, b, dims, preferred_element_type=F32)


def kernel(
    q_hbm, k_hbm, v_hbm, g_hbm, w_hbm, len_hbm, strata_hbm, level_hbm,
    dq_out, dk_out, dv_out, dw_out,
    len_ref, strata_ref, level_ref,
    q_all, k_all, v_all, g_all, w_all, dacc, do_all, p_all, o_all, s_all,
    dq_all, dkv_own, o_ret, ret1, ret1_in, ret2, ret2_in, part, part_in,
    parts, zs, zr, xs0, xr0, xs1, xr1, totals, z_sum, z_out, z_in, x_out, x_in, total,
    local_sem, ag_send, ag_recv, sib_send, sib_recv, kv_send, kv_recv,
    ret_send, ret_recv, z_send, z_recv, x_send, x_recv, far_send, far_recv,
):
    c = lax.axis_index("ctx")
    h = lax.axis_index("head")
    z, x, y, core = c // NX, c % NX, h // 2, h % 2
    side = c % 2
    sign = 2 * side - 1
    edge = pl.multiple_of(side * (TOK - HALO), HALO)

    def at_ctx(index):
        return {"ctx": (index + NZ * NX) % (NZ * NX), "head": h}

    def at_zx(zz, xx):
        return {"ctx": (zz + NZ) % NZ * NX + (xx + NX) % NX, "head": h}

    def at_y(yy, k):
        return {"ctx": c, "head": (yy + NY) % NY * 2 + k}

    z_up, z_dn = at_zx(z + 1, x), at_zx(z - 1, x)
    x_up, x_dn = at_zx(z, x + 1), at_zx(z, x - 1)
    sibling = {"ctx": c, "head": h + 1 - 2 * core}
    partner = at_ctx(c - sign)
    mirror = at_ctx(c + sign)
    far_to, far_from = at_ctx(c + 2 * sign), at_ctx(c - 2 * sign)

    def remote(src, dst, ssem, rsem, device):
        return pltpu.make_async_remote_copy(
            src_ref=src, dst_ref=dst, send_sem=ssem, recv_sem=rsem, device_id=device, device_id_type=MESH
        )

    barrier = pltpu.get_barrier_semaphore()
    greeted = [at_y(y + d, k) for d in (1, -1) for k in range(2)] + [sibling, partner, mirror, far_to, far_from]
    greeted += [at_zx(z, x + d) for d in range(1, NX)] + [at_zx(z + d, x) for d in (1, 2, -2, -1)]
    for device in greeted:
        pl.semaphore_signal(barrier, inc=1, device_id=device, device_id_type=MESH)

    own = [
        pltpu.make_async_copy(src, dst, local_sem.at[n])
        for n, (src, dst) in enumerate(
            [
                (len_hbm, len_ref),
                (strata_hbm, strata_ref),
                (level_hbm, level_ref),
                (g_hbm, g_all.at[0, core]),
                (q_hbm, q_all.at[pl.ds(0, TOK)]),
                (k_hbm, k_all.at[pl.ds(0, TOK)]),
                (v_hbm, v_all.at[pl.ds(0, TOK)]),
                (w_hbm, w_all),
            ]
        )
    ]
    for copy in own:
        copy.start()

    pl.semaphore_wait(barrier, len(greeted))

    chunk = TOK // 8

    def chunk_at(p, k):
        return pl.ds(pl.multiple_of((p + 4 * k) % 8 * chunk, chunk), chunk)

    ag = []

    def ag_first(p, up):
        rows_of = chunk_at(p, 0 if up else 1)
        copy = remote(
            g_hbm.at[rows_of], g_all.at[NY - 1 if up else 1, core, rows_of],
            ag_send.at[p if up else 8 + p], ag_recv.at[core * 8 + p],
            at_y(y + 1, 0) if up else at_y(y - 1, 1),
        )
        copy.start()
        ag.append(copy)

    onward = at_y(y + 1 - 2 * core, core)

    def slot_at(s):
        return (NY + (2 * core - 1) * s) % NY

    def ag_copy(s, k, p):
        rows_of = chunk_at(p, core)
        index = 16 * s + 8 * k + p
        return remote(
            g_all.at[slot_at(s), k, rows_of], g_all.at[slot_at(s + 1), k, rows_of],
            ag_send.at[index], ag_recv.at[index], onward,
        )

    def ag_arrival(s, k, p):
        rows_of = chunk_at(p, core)
        index = 16 * (s - 1) + 8 * k + p
        here = g_all.at[slot_at(s), k, rows_of]
        remote(here, here, ag_send.at[index], ag_recv.at[index], onward).wait_recv()

    for p in range(8):
        for up in (True, False):
            ag_first(p, up)
    kv = [
        remote(k_hbm, k_all.at[pl.ds(TOK, TOK)], kv_send.at[0], kv_recv.at[0], partner),
        remote(v_hbm, v_all.at[pl.ds(TOK, TOK)], kv_send.at[1], kv_recv.at[1], partner),
    ]
    rim = pl.ds(edge, HALO)
    for n, (src, dst, device) in enumerate(
        [
            (k_hbm, k_all.at[pl.ds(2 * TOK, HALO)], mirror),
            (v_hbm, v_all.at[pl.ds(2 * TOK, HALO)], mirror),
            (q_hbm, q_all.at[pl.ds(TOK, HALO)], mirror),
            (k_hbm, k_all.at[pl.ds(2 * TOK + HALO, HALO)], far_to),
            (v_hbm, v_all.at[pl.ds(2 * TOK + HALO, HALO)], far_to),
        ]
    ):
        kv.append(remote(src.at[rim], dst, kv_send.at[2 + n], kv_recv.at[2 + n], device))
    for copy in kv[2:] + kv[:2]:
        copy.start()
    sib = []

    def pass_on(s):
        if s == 0:
            src, dst = g_hbm, g_all.at[0, core]
        elif s < NY // 2:
            src = dst = g_all.at[slot_at(s)]
        else:
            src = dst = g_all.at[s, :, pl.ds(pl.multiple_of(core * (TOK // 2), TOK // 2), TOK // 2)]
        copy = remote(src, dst, sib_send.at[s], sib_recv.at[s], sibling)
        copy.start()
        sib.append(copy)

    def from_sibling(s):
        if s == 0:
            here = g_all.at[0, 1 - core]
        elif s < NY // 2:
            here = g_all.at[slot_at(-s)]
        else:
            here = g_all.at[s, :, pl.ds(pl.multiple_of((1 - core) * (TOK // 2), TOK // 2), TOK // 2)]
        remote(here, here, sib_send.at[s], sib_recv.at[s], sibling).wait_recv()

    pass_on(0)

    for copy in own:
        copy.wait()

    doc = c // 2
    position = c * TOK + lax.broadcasted_iota(jnp.int32, (1, TOK), 1)
    stratum = jnp.zeros((1, TOK), jnp.int32)
    begin = jnp.int32(0)
    doc_begin = jnp.int32(0)
    doc_end = jnp.int32(0)
    for n in range(16):
        finish = begin + len_ref[n]
        within = (position >= begin) & (position < finish)
        stratum = jnp.where(within, strata_ref[n], stratum)
        doc_begin = jnp.where(doc == n, begin, doc_begin)
        doc_end = jnp.where(doc == n, finish, doc_end)
        begin = finish
    level = level_ref[...].reshape(1, TOK)
    weight_row = jnp.where(level < stratum + 1, STRATA / (stratum + 1).astype(F32), 0.0)
    weight = jnp.transpose(jnp.broadcast_to(weight_row, (HD, TOK)))

    other = 1 - side

    def place(index, own_first, halo_first):
        return jnp.where(index < TOK, own_first + index, halo_first + index - TOK)

    own_first = c * TOK
    own_halo = own_first - HALO + (TOK + HALO) * side
    partner_first = (c - sign) * TOK
    partner_halo = partner_first - HALO + (TOK + HALO) * other
    rows = place(lax.broadcasted_iota(jnp.int32, (EXT, 1), 0), own_first, own_halo)
    row_in = ((rows >= doc_begin) & (rows < doc_end)).astype(F32)
    lane = lax.broadcasted_iota(jnp.int32, (1, KEYS), 1)
    keys_at = jnp.where(
        lane < TOK,
        own_first + lane,
        jnp.where(
            lane < 2 * TOK,
            partner_first + lane - TOK,
            jnp.where(lane < 2 * TOK + HALO, own_halo + lane - 2 * TOK, partner_halo + lane - 2 * TOK - HALO),
        ),
    )
    key_in = (keys_at >= doc_begin) & (keys_at < doc_end) & (lane < 2 * TOK + 2 * HALO)
    bias = jnp.where(key_in, 0.0, NEG)
    pad = KEYS - 2 * TOK - 2 * HALO
    k_all[pl.ds(KEYS - pad, pad), :] = jnp.zeros((pad, COLS), BF16)
    v_all[pl.ds(KEYS - pad, pad), :] = jnp.zeros((pad, COLS), BF16)

    def ag_step(s):
        for p in range(8 if s < NY // 2 else 4):
            for k in range(2):
                ag_arrival(s, k, p)
                if s < NY // 2 and (s + 1 < NY // 2 or p < 4):
                    copy = ag_copy(s, k, p)
                    copy.start()
                    ag.append(copy)
        pass_on(s)

    ag_step(1)
    ag_step(2)

    scale = HD**-0.5
    for copy in kv:
        copy.wait_recv()

    def forward(n, first, count):
        rows_of, cols = pl.ds(first, count), pl.ds(n * HD, HD)
        scores = dot(q_all[rows_of, cols], k_all[:, cols], NT) * scale + bias
        top = jnp.max(scores, axis=1, keepdims=True)
        terms = jnp.exp(scores - top)
        attention = terms * (row_in[first : first + count] / jnp.sum(terms, axis=1, keepdims=True))
        p_all[n, rows_of, :] = attention
        o_all[rows_of, cols] = dot(attention.astype(BF16), v_all[:, cols])

    forward(0, TOK, HALO)
    forward(1, TOK, HALO)
    back = remote(o_all.at[pl.ds(TOK, HALO)], o_ret, ret_send.at[0], ret_recv.at[0], mirror)
    back.start()
    forward(0, 0, TOK)
    forward(1, 0, TOK)

    ag_step(3)
    ag_step(NY // 2)

    back.wait_recv()
    s_all[...] = o_all[pl.ds(0, TOK), :]
    s_all[rim, :] += o_ret[...]
    for n in range(2):
        cols = pl.ds(n * HD, HD)
        s_all[:, cols] = s_all[:, cols] * weight
    scaled = s_all[...].astype(BF16)

    spots = [(x + 2) % NX, (x + 1) % NX, (x + NX - 1) % NX, x]

    def make_part(d):
        for r in range(2):
            first = (y + d) % NY * (2 * COLS) + r * COLS
            parts[pl.ds(pl.multiple_of(first, COLS), COLS), :] = dot(g_all[d, r], scaled, TN)

    def part_z(e, q):
        first = (z + e) % NZ * (NX * DEST) + spots[q] * DEST
        return parts[pl.ds(pl.multiple_of(first, DEST), ROWS_Z), :]

    def part_x(d, q):
        first = (y + d) % NY * (NX * DEST) + spots[q] * DEST + ROWS_Z
        return parts[pl.ds(pl.multiple_of(first, 16), ROWS_X), :]

    zc = {}

    def z_send_group(up, t, late):
        e = 4 - t if up else (4 + t) % NZ
        d, group = 0 if up else 1, 0 if up != late else 1
        came = zc.get((up, t - 1, late))
        if came is not None:
            came.wait_recv()
        for n in range(2):
            value = part_z(e, group * 2 + n)
            if came is not None:
                value = value + zr[d, t - 1, group, n].astype(F32)
            zs[d, t, group, n] = value.astype(BF16)
        index = d * 8 + t * 2 + group
        copy = remote(
            zs.at[d, t, group], zr.at[d, t, group], z_send.at[index], z_recv.at[index], z_up if up else z_dn
        )
        copy.start()
        zc[up, t, late] = copy

    def z_first(t):
        z_send_group(True, t, False)
        z_send_group(False, t, False)

    def z_second(t):
        z_send_group(True, t, True)
        z_send_group(False, t, True)

    xc = {}
    pairs = ((0, 1), (7, 2), (6, 3), (5, 4))

    def x_start(u):
        for n, up in enumerate((True, False)):
            xs0[u, n] = part_x(pairs[u][n], 0).astype(BF16)
            index = u * 2 + n
            xc[up, 0, u] = remote(
                xs0.at[u, n], xr0.at[u, n], x_send.at[index], x_recv.at[index], x_up if up else x_dn
            )
            xc[up, 0, u].start()

    def x_next(u):
        for n, up in enumerate((True, False)):
            for m in range(2):
                value = part_x(pairs[u][m], 1 if up else 2)
                if m == n:
                    xc[up, 0, u].wait_recv()
                    value = value + xr0[u, n].astype(F32)
                xs1[u, n, m] = value.astype(BF16)
            index = 8 + u * 2 + n
            xc[up, 1, u] = remote(
                xs1.at[u, n], xr1.at[u, n], x_send.at[index], x_recv.at[index], x_up if up else x_dn
            )
            xc[up, 1, u].start()

    def x_total(u):
        for up in (True, False):
            xc[up, 1, u].wait_recv()
        for m, d in enumerate(pairs[u]):
            totals[(y + d) % NY] = part_x(d, 3) + xr1[u, 0, m].astype(F32) + xr1[u, 1, m].astype(F32)

    straight = []

    def over_z(n, e, first, count, hop, *more):
        value = totals[(z + e) % NZ, first : first + count]
        for slot in more:
            straight[slot].wait_recv()
            if slot < 2:
                here = slice(0, ROWS_X // 2) if slot == 0 else slice(ROWS_X // 2, ROWS_X)
                z_sum[...] = value
                z_sum[here] += z_in[slot, : ROWS_X // 2].astype(F32)
                value = z_sum[...]
            else:
                value = value + z_in[slot].astype(F32)
        z_out[n, :count] = value.astype(BF16)
        here = pl.ds(0, count)
        copy = remote(
            z_out.at[n, here], z_in.at[n, here], far_send.at[n], far_recv.at[n], at_zx(z + hop, x)
        )
        copy.start()
        straight.append(copy)

    for s in range(3):
        from_sibling(s)
    for d in (0, 1, 7, 2):
        make_part(d)
    x_start(0)
    x_start(1)
    from_sibling(3)
    for d in (6, 3):
        make_part(d)
    x_start(2)
    make_part(5)

    def grad_block(slot):
        value = None
        for r in range(2):
            first = (y + slot) % NY * (2 * COLS) + r * COLS
            term = dot(g_all[slot, r], w_all[pl.ds(pl.multiple_of(first, COLS), COLS), :])
            value = term if value is None else value + term
        return value

    dacc[...] = grad_block(0)
    for slot in (1, 7, 2, 6, 3, 5):
        dacc[...] += grad_block(slot)

    from_sibling(NY // 2)
    make_part(4)
    z_first(0)
    x_start(3)
    z_second(1)

    dacc[...] += grad_block(4)
    for n in range(2):
        cols = pl.ds(n * HD, HD)
        do_all[pl.ds(0, TOK), cols] = (dacc[:, cols] * weight).astype(BF16)
    halo_grad = remote(
        do_all.at[rim], do_all.at[pl.ds(TOK, HALO)], ret_send.at[1], ret_recv.at[1], mirror
    )
    halo_grad.start()

    x_next(0)
    x_next(1)
    z_first(1)
    x_next(2)
    z_second(2)
    x_next(3)

    halo_grad.wait_recv()

    def backward(n):
        cols = pl.ds(n * HD, HD)
        attention = p_all[n]
        grads = do_all[:, cols]
        correction = jnp.sum(grads.astype(F32) * o_all[:, cols], axis=1, keepdims=True)
        dots = dot(grads, v_all[:, cols], NT)
        score_grad = (attention * (dots - correction) * scale).astype(BF16)
        dq_all[:, cols] = dot(score_grad, k_all[:, cols])
        for which, value in enumerate(
            (dot(score_grad, q_all[:, cols], TN), dot(attention.astype(BF16), grads, TN))
        ):
            dkv_own[which, :, cols] = value[:TOK]
            part[which, :, cols] = value[TOK : 2 * TOK].astype(BF16)
            ret1[1 + which, :, cols] = value[2 * TOK : 2 * TOK + HALO]
            ret2[which, :, cols] = value[2 * TOK + HALO : 2 * TOK + 2 * HALO]

    backward(0)
    z_first(2)
    backward(1)
    ret1[0] = dq_all[pl.ds(TOK, HALO), :]
    returns = [
        remote(part, part_in, ret_send.at[2], ret_recv.at[2], partner),
        remote(ret1, ret1_in, ret_send.at[3], ret_recv.at[3], mirror),
        remote(ret2, ret2_in, ret_send.at[4], ret_recv.at[4], far_from),
    ]
    for copy in returns:
        copy.start()

    z_second(3)
    for u in range(4):
        x_total(u)
    mid = ROWS_X // 2
    over_z(0, 4, 0, mid, 2)
    over_z(1, 4, mid, mid, -2)
    over_z(2, 3, 0, ROWS_X, 1)
    over_z(3, 5, 0, ROWS_X, -1)
    z_first(3)
    over_z(4, 1, 0, ROWS_X, 1)
    over_z(5, 7, 0, ROWS_X, -1)
    over_z(6, 2, 0, ROWS_X, 2, 0, 2)
    over_z(7, 6, 0, ROWS_X, -2, 1, 3)
    total[pl.ds(ROWS_Z, ROWS_X), :] = totals[z]

    def z_total(q):
        value = part_z(0, q)
        for d, up in ((0, True), (1, False)):
            late = (q >= 2) == up
            if (d, q // 2) not in arrived:
                zc[up, 3, late].wait_recv()
                arrived.add((d, q // 2))
            value = value + zr[d, 3, q // 2, q % 2].astype(F32)
        return value

    arrived = set()
    for q, d in ((0, 2), (1, 1), (2, NX - 1)):
        x_out[q] = z_total(q).astype(BF16)
        copy = remote(x_out.at[q], x_in.at[q], far_send.at[NZ + q], far_recv.at[NZ + q], at_zx(z, x + d))
        copy.start()
        straight.append(copy)
    total[pl.ds(0, ROWS_Z), :] = z_total(3)

    for copy in returns:
        copy.wait_recv()
    dq_all[rim, :] += ret1_in[0]
    dq_out[...] = dq_all[pl.ds(0, TOK), :].astype(BF16)
    for which, out in enumerate((dk_out, dv_out)):
        dkv_own[which, rim, :] += ret1_in[1 + which] + ret2_in[which]
        out[...] = (dkv_own[which] + part_in[which].astype(F32)).astype(BF16)

    for copy in straight[4:]:
        copy.wait_recv()
    for n in range(4, NZ):
        total[pl.ds(ROWS_Z, ROWS_X), :] += z_in[n].astype(F32)
    for q in range(3):
        total[pl.ds(0, ROWS_Z), :] += x_in[q].astype(F32)
    dw_out[...] = total[...]

    for copy in ag + sib + kv + [back, halo_grad] + returns + list(zc.values()):
        copy.wait_send()
    for copy in list(xc.values()) + straight:
        copy.wait_send()


def tail(*refs):
    count = len(refs) // 2
    sems = refs[-1]
    copies = [pltpu.make_async_copy(refs[n], refs[count + n], sems.at[n]) for n in range(count)]
    for copy in copies:
        copy.start()
    for copy in copies:
        copy.wait()


def local(queries, keys, values, grad_out, out_weight, doc_lengths, strata, mask_level):
    hbm = pl.BlockSpec(memory_space=pl.ANY)
    vmem = pl.BlockSpec(memory_space=pltpu.VMEM)
    dma = pltpu.SemaphoreType.DMA
    V = pltpu.VMEM
    outs = pl.pallas_call(
        kernel,
        out_shape=[
            V((TOK, COLS), BF16),
            V((TOK, COLS), BF16),
            V((TOK, COLS), BF16),
            V((DEST, COLS), F32),
        ],
        in_specs=[hbm] * 8,
        out_specs=[vmem] * 4,
        scratch_shapes=[
            pltpu.SMEM((16,), jnp.int32),
            pltpu.SMEM((16,), jnp.int32),
            V((TOK,), jnp.int32),
            V((EXT, COLS), BF16),
            V((KEYS, COLS), BF16),
            V((KEYS, COLS), BF16),
            V((NY, 2, TOK, COLS), BF16),
            V((4096, COLS), BF16),
            V((TOK, COLS), F32),
            V((EXT, COLS), BF16),
            V((2, EXT, KEYS), F32),
            V((EXT, COLS), F32),
            V((TOK, COLS), F32),
            V((EXT, COLS), F32),
            V((2, TOK, COLS), F32),
            V((HALO, COLS), F32),
            V((3, HALO, COLS), F32),
            V((3, HALO, COLS), F32),
            V((2, HALO, COLS), F32),
            V((2, HALO, COLS), F32),
            V((2, TOK, COLS), BF16),
            V((2, TOK, COLS), BF16),
            V((NZ * NX * DEST, COLS), F32),
            V((2, 4, 2, 2, ROWS_Z, COLS), BF16),
            V((2, 4, 2, 2, ROWS_Z, COLS), BF16),
            V((4, 2, ROWS_X, COLS), BF16),
            V((4, 2, ROWS_X, COLS), BF16),
            V((4, 2, 2, ROWS_X, COLS), BF16),
            V((4, 2, 2, ROWS_X, COLS), BF16),
            V((NZ, ROWS_X, COLS), F32),
            V((ROWS_X, COLS), F32),
            V((NZ, ROWS_X, COLS), BF16),
            V((NZ, ROWS_X, COLS), BF16),
            V((3, ROWS_Z, COLS), BF16),
            V((3, ROWS_Z, COLS), BF16),
            V((DEST, COLS), F32),
            dma((8,)),
            dma((64,)),
            dma((64,)),
            dma((5,)),
            dma((5,)),
            dma((7,)),
            dma((7,)),
            dma((5,)),
            dma((5,)),
            dma((16,)),
            dma((16,)),
            dma((16,)),
            dma((16,)),
            dma((NZ + 3,)),
            dma((NZ + 3,)),
        ],
        compiler_params=pltpu.CompilerParams(
            collective_id=0, has_side_effects=True, vmem_limit_bytes=60 * 2**20
        ),
    )(queries, keys, values, grad_out, out_weight, doc_lengths, strata, mask_level)
    return pl.pallas_call(
        tail,
        out_shape=[jax.ShapeDtypeStruct(a.shape, a.dtype) for a in outs],
        in_specs=[vmem] * 4,
        out_specs=[hbm] * 4,
        scratch_shapes=[dma((4,))],
        compiler_params=pltpu.CompilerParams(vmem_limit_bytes=8 * 2**20),
    )(*outs)


def solution(mesh):
    placed = (
        P("ctx", "head"),
        P("ctx", "head"),
        P("ctx", "head"),
        P("ctx", "head"),
        P(None, "head"),
        P(),
        P(),
        P("ctx"),
    )
    return jax.shard_map(
        local,
        mesh=mesh,
        in_specs=placed,
        out_specs=(P("ctx", "head"), P("ctx", "head"), P("ctx", "head"), P("ctx", "head")),
        check_vma=False,
    )
```
